256 devices in a mesh: pool: 32 (over z, x), head: 8 (over y, core).
Axes of the slice: x: 4, y: 4, z: 8, core: 2. Of those that a mesh axis runs over, the one named last changes fastest.
Arguments:
- query: bfloat16 [8, 8192], P(None, 'head'), may hold values from -240 to 240, as said below
- query_pos: int32 [8], replicated, may hold values from 65536 to 69631
- key_latent: bfloat16 [8, 65536, 160], P(None, 'pool'), may hold values from -12 to 12
- key_up: bfloat16 [160, 1024], P(None, 'head'), may hold values from -0.5 to 0.5
- value_cache: bfloat16 [65536, 8, 1024], P('pool', None, 'head'), may hold values from -48 to 48
- chosen: int32 [8, 1024], replicated, may hold values from 0 to 8191, as said below
- value_slot: int32 [65536], replicated, may hold values from 0 to 65535, as said below
- out_weight: bfloat16 [8192, 8192], P('head', 'pool'), may hold values from -0.0625 to 0.0625
Outputs:
- mixed_out: bfloat16 [8, 8192], P(None, ('pool', 'head'))
The draws below stay inside these ranges and needn't reach their ends.
Inputs may be any that keep to these rules, and one draw needn't show every extreme that they name: `query`: entries of the shown draw lie within -6 to 6; in general a row of one head may be scaled by up to 40. `chosen`: each row lists 1024 distinct blocks of one sequence. Block c has its latents on pool index c // 256. Of one row, at most 64 blocks fall on one pool index; in every draw one pool index receives exactly 64 blocks of every row. `value_slot`: A permutation of the storage slots; slot v lies on pool index v // 2048. Among all chosen blocks, at most 16 have their value slot on one pool index and their latents on one other (or the same) pool index; in every draw some latent-holding pool index gets exactly 16 from every storing pool index.
All inputs are finite; a program needn't handle non-finite values.
Results may differ from the reference program's by a relative error of at most 0.035.
Values may be sent and summed in bfloat16 or wider, within the bound.
No kernel may reach another device: no remote copies, remote signals or barrier semaphores. Data moves between devices by JAX's collectives and lax.ppermute only.
A program may use at most 128 MiB of HBM per device.

```python
import math
import jax
import jax.numpy as jnp
from jax import lax

D = 8192
H = 64
KVH = 8
HD = 128
RANK = 160
SPAN = 8
SEQS = 8
SPANS_DEV = 256
MOST = 64
SEL = 1024
CTX_SPANS = 8192
CTX = 65536
N_POOL = 32


def first_places(sorted_ids, entry_total):
    starts = jnp.searchsorted(sorted_ids, sorted_ids, side='left').astype(jnp.int32)
    return jnp.arange(entry_total, dtype=jnp.int32) - starts


def selection_plan(key):
    key = jax.random.fold_in(key, 101)
    random_subkeys = jax.random.split(key, 7)
    holder_load_count = jax.random.randint(random_subkeys[0], (SEQS, N_POOL, 1), 0, 4) * 65536
    random_jitter = jax.random.randint(random_subkeys[1], (SEQS, N_POOL, MOST), 0, 65536)
    rank_load_penalty = (MOST - 1 - jnp.arange(MOST, dtype=jnp.int32)) * 1024
    forced_choice = jax.random.randint(random_subkeys[2], (), 0, N_POOL)
    forced_score_boost = jnp.where(jnp.arange(N_POOL, dtype=jnp.int32) == forced_choice, 1 << 19, 0)[None, :, None]
    block_scores = holder_load_count + random_jitter + rank_load_penalty[None, None, :] + forced_score_boost
    flat_scores = block_scores.reshape(SEQS, N_POOL * MOST) * (N_POOL * MOST) + jnp.arange(N_POOL * MOST, dtype=jnp.int32)[None, :]
    top_scores, picked_blocks = lax.top_k(flat_scores, SEL)
    holder = (picked_blocks // MOST).astype(jnp.int32)
    slot_rank = (picked_blocks % MOST).astype(jnp.int32)
    order_keys = jax.random.randint(random_subkeys[3], (SEQS, N_POOL, SPANS_DEV), 0, 1 << 20) * SPANS_DEV + jnp.arange(SPANS_DEV, dtype=jnp.int32)
    local_perm = jnp.argsort(order_keys, axis=-1).astype(jnp.int32)
    seq_ids = jnp.arange(SEQS, dtype=jnp.int32)[:, None]
    local_span = local_perm[seq_ids, holder, slot_rank]
    chosen = holder * SPANS_DEV + local_span
    entry_total = SEQS * SEL
    flat_holder = holder.reshape(-1)
    shuffle = jax.random.randint(random_subkeys[4], (entry_total,), 0, 1 << 20)
    entry_order = jnp.argsort(flat_holder * (1 << 20) + shuffle, stable=True)
    within_sorted = first_places(flat_holder[entry_order], entry_total)
    within = jnp.zeros((entry_total,), jnp.int32).at[entry_order].set(within_sorted)
    capacity = SEQS * MOST // N_POOL
    owner_keys = jax.random.randint(random_subkeys[5], (N_POOL, N_POOL), 0, 1 << 20) * N_POOL + jnp.arange(N_POOL, dtype=jnp.int32)[None, :]
    owner_perm = jnp.argsort(owner_keys, axis=-1).astype(jnp.int32)
    owner_of = owner_perm[flat_holder, within // capacity]
    owner_order = jnp.argsort(owner_of, stable=True)
    own_sorted = first_places(owner_of[owner_order], entry_total)
    own_rank = jnp.zeros((entry_total,), jnp.int32).at[owner_order].set(own_sorted)
    slot_count = SEQS * SPANS_DEV
    span_total = SEQS * CTX_SPANS
    span_global = (seq_ids * CTX_SPANS + chosen).reshape(-1)
    chosen_slot = owner_of * slot_count + own_rank
    used_flag = jnp.zeros((span_total,), jnp.int32).at[span_global].set(1)
    per_owner = jnp.sum((owner_of[:, None] == jnp.arange(N_POOL, dtype=jnp.int32)[None, :]).astype(jnp.int32), axis=0)
    occupied = (jnp.arange(slot_count, dtype=jnp.int32)[None, :] < per_owner[:, None]).astype(jnp.int32).reshape(-1)
    free_slots = jnp.argsort(occupied, stable=True).astype(jnp.int32)
    filler = jax.random.randint(random_subkeys[6], (span_total,), 0, 1 << 20) + used_flag * (1 << 21)
    fill_order = jnp.argsort(filler, stable=True)
    slot_table = jnp.zeros((span_total,), jnp.int32).at[fill_order].set(free_slots)
    slot_table = slot_table.at[span_global].set(chosen_slot)
    return (chosen, slot_table)


def draw_chosen(key, part):
    chosen, slot_table = selection_plan(key)
    return chosen


def draw_value_slot(key, part):
    chosen, slot_table = selection_plan(key)
    return slot_table


def draw_query(key, part):
    key = jax.random.fold_in(key, 11)
    base_draw = jax.random.truncated_normal(key, -6.0, 6.0, (SEQS, H * HD), jnp.float32)
    return base_draw.astype(jnp.bfloat16)


def draw_key_latent(key, part):
    key = jax.random.fold_in(key, 23)
    base_draw = jax.random.truncated_normal(key, -6.0, 6.0, (SEQS, CTX, RANK), jnp.float32) * 2.0
    return base_draw.astype(jnp.bfloat16)


def place_ends(result, own_key, low, top_value):
    longest = result.shape.index(max(result.shape))
    spots = []
    for shift in (0, 1):
        where = [jax.random.randint(jax.random.fold_in(own_key, axis), (), 0, length) for axis, length in enumerate(result.shape)]
        where[longest] = (where[longest] + shift) % result.shape[longest]
        spots.append(tuple(where))
    return result.at[spots[0]].set(low).at[spots[1]].set(top_value)


def block_scale(stream_key, shape, pieces, low, top_value):
    loudness = 1.0
    for axis_at, parts in pieces:
        steps = jax.random.uniform(jax.random.fold_in(jax.random.fold_in(stream_key, 6), axis_at), (parts,), jnp.float32, low / len(pieces), top_value / len(pieces))
        loudness = loudness * jnp.repeat(jnp.exp(steps), shape[axis_at] // parts).reshape((-1,) + (1,) * (len(shape) - 1 - axis_at))
    return loudness


def normal_values(key, dims, deviation, limit, cuts=(), kind=jnp.bfloat16):
    entries = deviation * jax.random.normal(key, dims, jnp.float32)
    if cuts:
        entries = entries * block_scale(key, dims, cuts, -0.22, 0.18)
    return jnp.clip(entries, -limit, limit).astype(kind)


def setup_inputs(seed: int = 0) -> dict:
    streams_of = jax.random.split(jax.random.key(seed), 9)
    query = draw_query(jax.random.fold_in(streams_of[8], 71), 0)
    query_pos = place_ends(jax.random.randint(streams_of[1], (SEQS,), CTX, CTX + 4096), jax.random.fold_in(streams_of[1], 1), CTX, (CTX + 4096) - 1).astype(jnp.int32)
    key_latent = draw_key_latent(jax.random.fold_in(streams_of[8], 71), 0)
    key_up = normal_values(streams_of[3], (RANK, KVH * HD), RANK ** -0.5, 0.5, ((1, 8),))
    value_cache = normal_values(streams_of[4], (SEQS * CTX_SPANS, SPAN, KVH * HD), 8.0, 48.0, ((0, 32), (2, 8)))
    chosen = draw_chosen(jax.random.fold_in(streams_of[8], 71), 0)
    value_slot = draw_value_slot(jax.random.fold_in(streams_of[8], 71), 0)
    out_weight = normal_values(streams_of[7], (H * HD, D), (H * HD) ** -0.5, 0.0625, ((0, 8), (1, 32)))
    return {"query": query, "query_pos": query_pos, "key_latent": key_latent, "key_up": key_up, "value_cache": value_cache, "chosen": chosen, "value_slot": value_slot, "out_weight": out_weight}


theta_base = 500000.0

def rotate(values, positions):
    half_width = values.shape[-1] // 2
    freq_index = jnp.arange(half_width, dtype=jnp.float32)
    inverse_freq = jnp.exp(-(2.0 * freq_index / values.shape[-1]) * math.log(theta_base))
    angles = positions.astype(jnp.float32)[..., None] * inverse_freq
    cosine = jnp.cos(angles)
    sine_part = jnp.sin(angles)
    first_half = values[..., :half_width]
    second = values[..., half_width:]
    return jnp.concatenate([first_half * cosine - second * sine_part, second * cosine + first_half * sine_part], axis=-1)

def reference(query, query_pos, key_latent, key_up, value_cache, chosen, value_slot, out_weight):
    group_size = H // KVH
    score_scale = 1.0 / math.sqrt(HD)

    def one_sequence(carried):
        query_row, position, latent_rows, span_ids, seq_index = carried
        token_ids = (span_ids[:, None] * SPAN + jnp.arange(SPAN, dtype=jnp.int32)[None, :]).reshape(-1)
        rebuilt = jnp.dot(latent_rows[token_ids], key_up, preferred_element_type=jnp.float32)
        rebuilt = rebuilt.reshape(-1, KVH, HD)
        key_rows = rotate(rebuilt, token_ids[:, None]).astype(jnp.bfloat16)
        queries = rotate(query_row.astype(jnp.float32).reshape(KVH, group_size, HD), position).astype(jnp.bfloat16)
        block_scores = jnp.einsum('kgd,tkd->kgt', queries.astype(jnp.float32), key_rows.astype(jnp.float32)) * score_scale
        row_peak = lax.optimization_barrier(jnp.max(block_scores, axis=-1, keepdims=True))
        weights = jnp.exp(block_scores - row_peak).astype(jnp.bfloat16)
        totals = lax.optimization_barrier(jnp.sum(weights.astype(jnp.float32), axis=-1))
        slot_ids = value_slot[seq_index * CTX_SPANS + span_ids]
        values = value_cache[slot_ids].reshape(-1, KVH, HD)
        summed = jnp.einsum('kgt,tkd->kgd', weights.astype(jnp.float32), values.astype(jnp.float32))
        return (summed / totals[..., None]).reshape(-1).astype(jnp.bfloat16)
    attended = lax.map(one_sequence, (query, query_pos, key_latent, chosen, jnp.arange(SEQS, dtype=jnp.int32)))
    return jnp.dot(attended, out_weight, preferred_element_type=jnp.float32).astype(jnp.bfloat16)
```

```python
import math

import jax
import jax.numpy as jnp
import numpy as np
from jax import lax
from jax.experimental import pallas as pl
from jax.experimental.pallas import tpu as pltpu
from jax.sharding import PartitionSpec as P

SEQS = 8
HEADS = 8
HD = 128
HALF = HD // 2
RANK = 160
SPAN = 8
THETA = 500000.0
LANES = 128

POOLS = 32
CAP = 16
ROWS = POOLS * CAP
SPANS = 256
TOKENS = SPANS * SPAN
SLOTS = 2048
CHUNKS = SEQS * SPANS // LANES
BIG_NEG = -1e30

f32 = jnp.float32
bf16 = jnp.bfloat16

HI_ROWS, MID_ROWS, LO_ROWS = 40, 16, 128
MID_AT, LO_AT = HI_ROWS, HI_ROWS + MID_ROWS


def angle_tables():
    inverse = np.exp(-(2.0 * np.arange(HALF) / HD) * math.log(THETA))
    rows = np.concatenate([np.arange(HI_ROWS) * 2048.0, np.arange(MID_ROWS) * 128.0, np.arange(LO_ROWS) * 1.0])
    angles = rows[:, None] * inverse[None, :]
    row_table = np.concatenate([np.cos(angles), np.sin(angles)], axis=1).astype(np.float32)
    lanes = np.arange(LANES)
    columns = np.concatenate([np.minimum(lanes, HI_ROWS - 1) * 2048.0, np.minimum(lanes, MID_ROWS - 1) * 128.0, lanes * 1.0])
    angles = inverse[:, None] * columns[None, :]
    column_table = np.concatenate([np.cos(angles), np.sin(angles)], axis=0).astype(np.float32)
    return row_table, column_table


def iota(shape, dim):
    return lax.broadcasted_iota(jnp.int32, shape, dim)


def onehot(condition):
    return jnp.where(condition, 1.0, 0.0).astype(bf16)


def dot(a, b):
    return lax.dot_general(a, b, (((1,), (0,)), ((), ())), preferred_element_type=f32)


def dot_nt(a, b):
    return lax.dot_general(a, b, (((1,), (1,)), ((), ())), preferred_element_type=f32)


def pieces_of(x):
    first = x.astype(bf16).astype(f32)
    rest = x - first
    second = rest.astype(bf16).astype(f32)
    return first, second, rest - second


def rotate_queries(pos_ref, query_ref, row_ref, angle_scr, q_scr, q_out):
    for s in range(SEQS):
        pos = pos_ref[s]
        angle_scr[0, s : s + 1, :] = row_ref[pl.ds(pos >> 11, 1), :]
        angle_scr[1, s : s + 1, :] = row_ref[pl.ds(MID_AT + ((pos >> 7) & 15), 1), :]
        angle_scr[2, s : s + 1, :] = row_ref[pl.ds(LO_AT + (pos & 127), 1), :]
    first, second, third = angle_scr[0], angle_scr[1], angle_scr[2]
    cosine = first[:, :HALF] * second[:, :HALF] - first[:, HALF:] * second[:, HALF:]
    sine = first[:, HALF:] * second[:, :HALF] + first[:, :HALF] * second[:, HALF:]
    cosine, sine = (
        cosine * third[:, :HALF] - sine * third[:, HALF:],
        sine * third[:, :HALF] + cosine * third[:, HALF:],
    )
    for h in range(HEADS):
        rows = query_ref[:, h * HD : (h + 1) * HD].astype(f32)
        a, b = rows[:, :HALF], rows[:, HALF:]
        turned = jnp.concatenate([a * cosine - b * sine, b * cosine + a * sine], axis=1)
        q_scr[h * SEQS : (h + 1) * SEQS, :] = turned.astype(bf16).astype(f32)
    for s in range(SEQS):
        q_out[s] = q_scr[pl.ds(s, HEADS, stride=SEQS), :]


def key_angles(pool, column_ref, cos_scr, sin_scr):
    lane = iota((HD, LANES), 1)
    base = jnp.sum(jnp.where(lane == pool, column_ref[:, :LANES], 0.0), axis=1, keepdims=True)
    cp, sp = base[:HALF], base[HALF:]
    c2, s2 = column_ref[:HALF, LANES : 2 * LANES], column_ref[HALF:, LANES : 2 * LANES]
    cb, sb = cp * c2 - sp * s2, sp * c2 + cp * s2
    c3, s3 = column_ref[:HALF, 2 * LANES :], column_ref[HALF:, 2 * LANES :]
    for c in range(TOKENS // LANES):
        ca, sa = cb[:, c : c + 1], sb[:, c : c + 1]
        cos_scr[:, c * LANES : (c + 1) * LANES] = ca * c3 - sa * s3
        sin_scr[:, c * LANES : (c + 1) * LANES] = sa * c3 + ca * s3


def plan(pool, chosen_ref, slot_ref, slot_scr, span_scr, seq_scr, meta_scr):
    relative = chosen_ref[...] - pool * SPANS
    here = (relative >= 0) & (relative < SPANS)
    row_code = jnp.where(here, 2 * iota(relative.shape, 0) + (relative >> 7), -1)
    lane_code = relative & 127
    picks = relative.shape[1]
    member = jnp.zeros((CHUNKS, LANES), f32)
    for s in range(SEQS):
        left = onehot(iota((CHUNKS, picks), 0) == row_code[s : s + 1, :])
        right = onehot(iota((LANES, picks), 0) == lane_code[s : s + 1, :])
        member = member + dot_nt(left, right)
    for s in range(SEQS):
        slot_scr[2 * s : 2 * s + 2, :] = slot_ref[pl.ds(s * (SPANS * POOLS // LANES) + 2 * pool, 2), :]
    slots = slot_scr[...]
    owner = jnp.where(member > 0.5, slots >> 11, -1)
    local_slot = slots & (SLOTS - 1)
    owners = [jnp.where(iota((POOLS, LANES), 0) == owner[c : c + 1, :], 1.0, 0.0) for c in range(CHUNKS)]
    earlier = iota((LANES, 2 * LANES), 0) < iota((LANES, 2 * LANES), 1)
    counted = dot(jnp.concatenate(owners, axis=0).astype(bf16), onehot(earlier))
    carry = jnp.zeros((POOLS, LANES), f32)
    facts = []
    for c in range(CHUNKS):
        part = counted[c * POOLS : (c + 1) * POOLS]
        rank = jnp.sum(owners[c] * (part[:, :LANES] + carry), axis=0, keepdims=True).astype(jnp.int32)
        carry = carry + part[:, LANES:]
        at_rank = jnp.where(iota((CAP, LANES), 0) == rank, 1.0, 0.0)
        span = (iota((1, LANES), 1) + (c % 2) * LANES).astype(f32)
        slot = local_slot[c : c + 1, :]
        facts.append(
            jnp.concatenate(
                [
                    at_rank * span,
                    at_rank * float(c // 2 + 1),
                    at_rank * (slot >> 6).astype(f32),
                    at_rank * (slot & 63).astype(f32),
                ],
                axis=0,
            )
        )
    table = dot_nt(
        jnp.concatenate(owners, axis=1).astype(bf16), jnp.concatenate(facts, axis=1).astype(bf16)
    )
    spread = dot(onehot((iota((ROWS, POOLS), 0) >> 4) == iota((ROWS, POOLS), 1)), table.astype(bf16))
    own = (iota(spread.shape, 1) & (CAP - 1)) == (iota(spread.shape, 0) & (CAP - 1))
    kind = iota((4 * CAP, 3 * LANES), 0) >> 4
    column = iota((4 * CAP, 3 * LANES), 1)
    fold = onehot(
        ((column < LANES) & (kind == 0))
        | ((column >= LANES) & (column < 2 * LANES) & (kind == 1))
        | ((column == 2 * LANES + 88) & (kind == 2))
        | ((column == 2 * LANES + 89) & (kind == 3))
        | ((column == 2 * LANES + 90) & (kind == 1))
    )
    known = dot(jnp.where(own, spread, 0.0).astype(bf16), fold)
    span_scr[...] = known[:, :LANES]
    seq_scr[...] = known[:, LANES : 2 * LANES]
    meta_scr[...] = known[:, 2 * LANES :]


def pack_rows(score_scr, turned_scr, span_scr, seq_scr, meta_scr, out_ref):
    scores = score_scr[...]
    first = scores.astype(bf16).astype(f32)
    turned_scr[...] = jnp.concatenate([first, scores - first], axis=0).T
    parts = [turned_scr[pl.ds(t, SPANS, stride=SPAN), :].astype(bf16) for t in range(SPAN)]
    by_span = jnp.concatenate(parts, axis=1)
    width = SPAN * LANES
    source = iota((width, LANES), 0)
    target = iota((width, LANES), 1)
    fold = onehot(((source >> 7) == ((target & 63) >> 3)) & ((source & 7) == (target & 7)))
    block = 128
    lane = iota((block, LANES), 1)
    lane_seq = ((lane & 63) >> 3).astype(f32) + 1.0
    for start in range(0, ROWS, block):
        span = span_scr[start : start + block, :]
        seq = seq_scr[start : start + block, :]
        pick = jnp.concatenate([onehot(lane.astype(f32) == span), onehot((lane + LANES).astype(f32) == span)], axis=1)
        found = dot(pick, by_span)
        mine = seq == lane_seq
        kept = [jnp.where(mine, found[:, t * LANES : (t + 1) * LANES], 0.0) for t in range(SPAN)]
        score = dot(jnp.concatenate(kept, axis=1).astype(bf16), fold) * (1.0 / math.sqrt(HD))
        peak = score
        for shift in (8, 16, 32):
            peak = jnp.maximum(peak, pltpu.roll(peak, shift, 1))
        weight = jnp.where(seq > 0.5, jnp.exp(score - peak), 0.0)
        one, two, three = pieces_of(peak)
        packed = jnp.where(lane < 88, three, meta_scr[start : start + block, :])
        packed = jnp.where(lane < 80, two, packed)
        packed = jnp.where(lane < 72, one, packed)
        packed = jnp.where(lane < 64, weight, packed)
        out_ref[start : start + block, :] = packed.astype(bf16)


def holder_kernel(
    pos_hbm, query_hbm, latent_hbm, key_up_hbm, chosen_hbm, slot_hbm, row_hbm, column_hbm, out_ref,
    pos_ref, query_ref, latent_ref, key_up_ref, chosen_ref, slot_ref, row_ref, column_ref, sems,
    angle_scr, q_scr, q_out, up_scr, cos_scr, sin_scr, slot_scr, span_scr, seq_scr, meta_scr, score_scr, turned_scr,
):
    small = [
        pltpu.make_async_copy(source, target, sems.at[i])
        for i, (source, target) in enumerate(
            [
                (chosen_hbm, chosen_ref),
                (slot_hbm, slot_ref),
                (pos_hbm, pos_ref),
                (row_hbm, row_ref),
                (column_hbm, column_ref),
                (query_hbm, query_ref),
                (key_up_hbm, key_up_ref),
            ]
        )
    ]
    for copy in small:
        copy.start()
    latents = [pltpu.make_async_copy(latent_hbm.at[s], latent_ref.at[s], sems.at[len(small) + s]) for s in range(SEQS)]
    for copy in latents:
        copy.start()
    for copy in small:
        copy.wait()
    pool = lax.axis_index("pool")
    plan(pool, chosen_ref, slot_ref, slot_scr, span_scr, seq_scr, meta_scr)
    rotate_queries(pos_ref, query_ref, row_ref, angle_scr, q_scr, q_out)
    key_angles(pool, column_ref, cos_scr, sin_scr)
    up_scr[...] = key_up_ref[...].astype(f32).T.astype(bf16)
    score_all(latents, latent_ref, up_scr, q_out, cos_scr, sin_scr, score_scr)
    pack_rows(score_scr, turned_scr, span_scr, seq_scr, meta_scr, out_ref)


def score_all(latents, latent_ref, up_scr, q_out, cos_scr, sin_scr, score_scr):
    up = up_scr[...]
    cosine, sine = cos_scr[...], sin_scr[...]
    for s in range(SEQS):
        latents[s].wait()
        keys = dot(up, latent_ref[s])
        a, b = keys[:HALF], keys[HALF:]
        turned = jnp.concatenate([a * cosine - b * sine, b * cosine + a * sine], axis=0).astype(bf16)
        score_scr[s * HEADS : (s + 1) * HEADS, :] = dot(q_out[s].astype(bf16), turned)


def owner_kernel(
    packed_ref, values_ref, out_ref, slot_vec, slot_sca, sem, found_scr, sum_scr, level_scr
):
    packed = packed_ref[...].astype(f32).T
    slot_vec[...] = (packed[88:89] * 64.0 + packed[89:90]).astype(jnp.int32)
    copy = pltpu.make_async_copy(slot_vec, slot_sca, sem)
    copy.start()
    seq = packed[90:91]
    live = seq > 0.5
    peak = jnp.where(live, packed[64:72] + packed[72:80] + packed[80:88], BIG_NEG)
    mine = [seq == float(s + 1) for s in range(SEQS)]
    tops = [jnp.max(jnp.where(mine[s], peak, BIG_NEG), axis=1, keepdims=True) for s in range(SEQS)]
    top = jnp.zeros_like(peak)
    for s in range(SEQS):
        top = jnp.where(mine[s], tops[s], top)
    factor = jnp.where(live, jnp.exp(peak - top), 0.0)
    weights = [(packed[t * HEADS : (t + 1) * HEADS] * factor).astype(bf16).astype(f32) for t in range(SPAN)]
    over_span = weights[0]
    for t in range(1, SPAN):
        over_span = over_span + weights[t]
    totals = jnp.concatenate(
        [jnp.sum(jnp.where(mine[s], over_span, 0.0), axis=1, keepdims=True) for s in range(SEQS)], axis=0
    )
    peaks = jnp.concatenate(tops, axis=0)
    copy.wait()

    @pl.loop(0, ROWS // 16)
    def _(step):
        for i in range(16):
            row = step * 16 + i
            found_scr[pl.ds(pl.multiple_of(row * SPAN, SPAN), SPAN), :] = values_ref[slot_sca[0, row]].astype(f32)

    summed = jnp.zeros((SEQS * HEADS, HD), f32)
    for t in range(SPAN):
        left = jnp.concatenate([jnp.where(mine[s], weights[t], 0.0) for s in range(SEQS)], axis=0).astype(bf16)
        right = found_scr[pl.ds(t, ROWS, stride=SPAN), :].astype(bf16)
        summed = summed + dot(left, right)
    some = totals > 0.0
    safe = jnp.where(some, totals, 1.0)
    sum_scr[...] = summed / safe
    level = jnp.where(some, peaks + jnp.log(safe), BIG_NEG)
    level_scr[...] = jnp.broadcast_to(level, level_scr.shape)
    lane = iota((SEQS, LANES), 1)
    tail = jnp.zeros((SEQS, LANES), f32)
    parts = []
    for h in range(HEADS):
        parts.append(sum_scr[pl.ds(h, SEQS, stride=HEADS), :])
        tail = jnp.where((lane & 7) == h, level_scr[pl.ds(h, SEQS, stride=HEADS), :], tail)
    one, two, three = pieces_of(tail)
    parts.append(jnp.where(lane < 8, one, jnp.where(lane < 16, two, jnp.where(lane < 24, three, 0.0))))
    result = jnp.concatenate(parts, axis=1).astype(bf16)
    for p in range(POOLS):
        out_ref[p] = result


def combine_kernel(gathered_ref, weight_ref, out_ref):
    levels = []
    for p in range(POOLS):
        tail = gathered_ref[p, :, HEADS * HD :].astype(f32)
        levels.append(tail + pltpu.roll(tail, LANES - 8, 1) + pltpu.roll(tail, LANES - 16, 1))
    top = levels[0]
    for p in range(1, POOLS):
        top = jnp.maximum(top, levels[p])
    shares = [jnp.exp(level - top) for level in levels]
    total = shares[0]
    for p in range(1, POOLS):
        total = total + shares[p]
    inverse = 1.0 / total
    sums = [jnp.zeros((SEQS, HD), f32) for _ in range(HEADS)]
    for p in range(POOLS):
        share = shares[p] * inverse
        for h in range(HEADS):
            sums[h] = sums[h] + share[:, h : h + 1] * gathered_ref[p, :, h * HD : (h + 1) * HD].astype(f32)
    attended = jnp.concatenate(sums, axis=1).astype(bf16)
    projected = dot(attended, weight_ref[...])
    groups = out_ref.shape[0]
    width = projected.shape[1] // groups
    for g in range(groups):
        at = g * width
        half = projected[:, at // LANES * LANES : (at // LANES + 1) * LANES]
        out_ref[g] = pltpu.roll(half, (LANES - at % LANES) % LANES, 1)


def finish_kernel(parts_ref, out_ref):
    total = parts_ref[0]
    for g in range(1, parts_ref.shape[0]):
        total = total + parts_ref[g]
    out_ref[...] = total[:, : out_ref.shape[1]].astype(bf16)


def score(*operands):
    buffers = [pltpu.SMEM(operands[0].shape, jnp.int32)]
    buffers += [pltpu.VMEM(x.shape, x.dtype) for x in operands[1:]]
    return pl.pallas_call(
        holder_kernel,
        in_specs=[pl.BlockSpec(memory_space=pltpu.HBM)] * len(operands),
        out_specs=pl.BlockSpec(memory_space=pltpu.VMEM),
        out_shape=jax.ShapeDtypeStruct((ROWS, LANES), bf16),
        scratch_shapes=[
            *buffers,
            pltpu.SemaphoreType.DMA((len(operands) - 1 + SEQS,)),
            pltpu.VMEM((3, SEQS, LANES), f32),
            pltpu.VMEM((SEQS * HEADS, HD), f32),
            pltpu.VMEM((SEQS, HEADS, HD), f32),
            pltpu.VMEM((HD, RANK), bf16),
            pltpu.VMEM((HALF, TOKENS), f32),
            pltpu.VMEM((HALF, TOKENS), f32),
            pltpu.VMEM((CHUNKS, LANES), jnp.int32),
            pltpu.VMEM((ROWS, LANES), f32),
            pltpu.VMEM((ROWS, LANES), f32),
            pltpu.VMEM((ROWS, LANES), f32),
            pltpu.VMEM((SEQS * HEADS, TOKENS), f32),
            pltpu.VMEM((TOKENS, LANES), f32),
        ],
        compiler_params=pltpu.CompilerParams(vmem_limit_bytes=63_400_000),
        name="score",
    )(*operands)


def weigh(packed, values):
    return pl.pallas_call(
        owner_kernel,
        in_specs=[pl.BlockSpec(memory_space=pltpu.VMEM)] * 2,
        out_specs=pl.BlockSpec(memory_space=pltpu.VMEM),
        out_shape=jax.ShapeDtypeStruct((POOLS, SEQS, (HEADS + 1) * HD), bf16),
        scratch_shapes=[
            pltpu.VMEM((1, ROWS), jnp.int32),
            pltpu.SMEM((1, ROWS), jnp.int32),
            pltpu.SemaphoreType.DMA,
            pltpu.VMEM((ROWS * SPAN, HD), f32),
            pltpu.VMEM((SEQS * HEADS, HD), f32),
            pltpu.VMEM((SEQS * HEADS, LANES), f32),
        ],
        compiler_params=pltpu.CompilerParams(vmem_limit_bytes=32 << 20),
        name="weigh",
    )(packed, values)


def combine(gathered, out_weight, groups):
    return pl.pallas_call(
        combine_kernel,
        in_specs=[pl.BlockSpec(memory_space=pltpu.VMEM)] * 2,
        out_specs=pl.BlockSpec(memory_space=pltpu.VMEM),
        out_shape=jax.ShapeDtypeStruct((groups, SEQS, LANES), f32),
        name="combine",
    )(gathered, out_weight)


def finish(parts, width):
    return pl.pallas_call(
        finish_kernel,
        in_specs=[pl.BlockSpec(memory_space=pltpu.VMEM)],
        out_specs=pl.BlockSpec(memory_space=pltpu.VMEM),
        out_shape=jax.ShapeDtypeStruct((SEQS, width), bf16),
        name="finish",
    )(parts)


def on_device(query, query_pos, key_latent, key_up, value_cache, chosen, value_slot, out_weight):
    row_table, column_table = angle_tables()
    latent = jnp.swapaxes(key_latent, 1, 2)
    slot_rows = value_slot.reshape(-1, LANES)
    packed = score(query_pos, query, latent, key_up, chosen, slot_rows, row_table, column_table)
    arrived = lax.all_to_all(packed.reshape(POOLS, CAP, LANES), "pool", split_axis=0, concat_axis=0, tiled=True)
    partial = weigh(arrived.reshape(ROWS, LANES), value_cache)
    gathered = lax.all_to_all(partial, "pool", split_axis=0, concat_axis=0, tiled=True)
    groups = lax.axis_size("head")
    projected = combine(gathered, out_weight, groups)
    parts = lax.all_to_all(projected, "head", split_axis=0, concat_axis=0, tiled=True)
    return finish(parts, out_weight.shape[1] // groups)


def solution(mesh):
    placed = (
        P(None, "head"),
        P(),
        P(None, "pool", None),
        P(None, "head"),
        P("pool", None, "head"),
        P(),
        P(),
        P("head", "pool"),
    )
    return jax.shard_map(
        on_device, mesh=mesh, in_specs=placed, out_specs=P(None, ("pool", "head")), check_vma=False
    )
```

```python
import math

import jax
import jax.numpy as jnp
import numpy as np
from jax import lax
from jax.experimental import pallas as pl
from jax.experimental.pallas import tpu as pltpu
from jax.sharding import PartitionSpec as P

SEQS = 8
HEADS = 8
HD = 128
HALF = HD // 2
RANK = 160
SPAN = 8
THETA = 500000.0
LANES = 128

POOLS = 32
CAP = 16
ROWS = POOLS * CAP
SPANS = 256
TOKENS = SPANS * SPAN
SLOTS = 2048
CHUNKS = SEQS * SPANS // LANES
BIG_NEG = -1e30

f32 = jnp.float32
bf16 = jnp.bfloat16

HI_ROWS, MID_ROWS, LO_ROWS = 40, 16, 128
MID_AT, LO_AT = HI_ROWS, HI_ROWS + MID_ROWS


def angle_tables():
    inverse = np.exp(-(2.0 * np.arange(HALF) / HD) * math.log(THETA))
    rows = np.concatenate([np.arange(HI_ROWS) * 2048.0, np.arange(MID_ROWS) * 128.0, np.arange(LO_ROWS) * 1.0])
    angles = rows[:, None] * inverse[None, :]
    row_table = np.concatenate([np.cos(angles), np.sin(angles)], axis=1).astype(np.float32)
    lanes = np.arange(LANES)
    columns = np.concatenate([np.minimum(lanes, HI_ROWS - 1) * 2048.0, np.minimum(lanes, MID_ROWS - 1) * 128.0, lanes * 1.0])
    angles = inverse[:, None] * columns[None, :]
    column_table = np.concatenate([np.cos(angles), np.sin(angles)], axis=0).astype(np.float32)
    return row_table, column_table


def iota(shape, dim):
    return lax.broadcasted_iota(jnp.int32, shape, dim)


def onehot(condition):
    return jnp.where(condition, 1.0, 0.0).astype(bf16)


def dot(a, b):
    return lax.dot_general(a, b, (((1,), (0,)), ((), ())), preferred_element_type=f32)


def dot_nt(a, b):
    return lax.dot_general(a, b, (((1,), (1,)), ((), ())), preferred_element_type=f32)


def pieces_of(x):
    first = x.astype(bf16).astype(f32)
    rest = x - first
    second = rest.astype(bf16).astype(f32)
    return first, second, rest - second


def rotate_queries(pos_ref, query_ref, row_ref, angle_scr, q_scr, q_out):
    for s in range(SEQS):
        pos = pos_ref[s]
        angle_scr[0, s : s + 1, :] = row_ref[pl.ds(pos >> 11, 1), :]
        angle_scr[1, s : s + 1, :] = row_ref[pl.ds(MID_AT + ((pos >> 7) & 15), 1), :]
        angle_scr[2, s : s + 1, :] = row_ref[pl.ds(LO_AT + (pos & 127), 1), :]
    first, second, third = angle_scr[0], angle_scr[1], angle_scr[2]
    cosine = first[:, :HALF] * second[:, :HALF] - first[:, HALF:] * second[:, HALF:]
    sine = first[:, HALF:] * second[:, :HALF] + first[:, :HALF] * second[:, HALF:]
    cosine, sine = (
        cosine * third[:, :HALF] - sine * third[:, HALF:],
        sine * third[:, :HALF] + cosine * third[:, HALF:],
    )
    for h in range(HEADS):
        rows = query_ref[:, h * HD : (h + 1) * HD].astype(f32)
        a, b = rows[:, :HALF], rows[:, HALF:]
        turned = jnp.concatenate([a * cosine - b * sine, b * cosine + a * sine], axis=1)
        q_scr[h * SEQS : (h + 1) * SEQS, :] = turned.astype(bf16).astype(f32)
    for s in range(SEQS):
        q_out[s] = q_scr[pl.ds(s, HEADS, stride=SEQS), :]


def key_angles(pool, column_ref, cos_scr, sin_scr):
    lane = iota((HD, LANES), 1)
    base = jnp.sum(jnp.where(lane == pool, column_ref[:, :LANES], 0.0), axis=1, keepdims=True)
    cp, sp = base[:HALF], base[HALF:]
    c2, s2 = column_ref[:HALF, LANES : 2 * LANES], column_ref[HALF:, LANES : 2 * LANES]
    cb, sb = cp * c2 - sp * s2, sp * c2 + cp * s2
    c3, s3 = column_ref[:HALF, 2 * LANES :], column_ref[HALF:, 2 * LANES :]
    for c in range(TOKENS // LANES):
        ca, sa = cb[:, c : c + 1], sb[:, c : c + 1]
        cos_scr[:, c * LANES : (c + 1) * LANES] = ca * c3 - sa * s3
        sin_scr[:, c * LANES : (c + 1) * LANES] = sa * c3 + ca * s3


def plan(pool, chosen_ref, slot_ref, slot_scr, span_scr, seq_scr, meta_scr, mask_scr):
    relative = chosen_ref[...] - pool * SPANS
    here = (relative >= 0) & (relative < SPANS)
    row_code = jnp.where(here, 2 * iota(relative.shape, 0) + (relative >> 7), -1)
    lane_code = relative & 127
    picks = relative.shape[1]
    member = jnp.zeros((CHUNKS, LANES), f32)
    for s in range(SEQS):
        left = onehot(iota((CHUNKS, picks), 0) == row_code[s : s + 1, :])
        right = onehot(iota((LANES, picks), 0) == lane_code[s : s + 1, :])
        member = member + dot_nt(left, right)
    mask_scr[...] = dot(member.astype(bf16), onehot(iota((LANES, LANES * SPAN), 0) == (iota((LANES, LANES * SPAN), 1) >> 3)))
    for s in range(SEQS):
        slot_scr[2 * s : 2 * s + 2, :] = slot_ref[pl.ds(s * (SPANS * POOLS // LANES) + 2 * pool, 2), :]
    slots = slot_scr[...]
    owner = jnp.where(member > 0.5, slots >> 11, -1)
    local_slot = slots & (SLOTS - 1)
    owners = [jnp.where(iota((POOLS, LANES), 0) == owner[c : c + 1, :], 1.0, 0.0) for c in range(CHUNKS)]
    earlier = iota((LANES, 2 * LANES), 0) < iota((LANES, 2 * LANES), 1)
    counted = dot(jnp.concatenate(owners, axis=0).astype(bf16), onehot(earlier))
    carry = jnp.zeros((POOLS, LANES), f32)
    facts = []
    for c in range(CHUNKS):
        part = counted[c * POOLS : (c + 1) * POOLS]
        rank = jnp.sum(owners[c] * (part[:, :LANES] + carry), axis=0, keepdims=True).astype(jnp.int32)
        carry = carry + part[:, LANES:]
        at_rank = jnp.where(iota((CAP, LANES), 0) == rank, 1.0, 0.0)
        span = (iota((1, LANES), 1) + (c % 2) * LANES).astype(f32)
        slot = local_slot[c : c + 1, :]
        facts.append(
            jnp.concatenate(
                [
                    at_rank * span,
                    at_rank * float(c // 2 + 1),
                    at_rank * (slot >> 6).astype(f32),
                    at_rank * (slot & 63).astype(f32),
                ],
                axis=0,
            )
        )
    table = dot_nt(
        jnp.concatenate(owners, axis=1).astype(bf16), jnp.concatenate(facts, axis=1).astype(bf16)
    )
    spread = dot(onehot((iota((ROWS, POOLS), 0) >> 4) == iota((ROWS, POOLS), 1)), table.astype(bf16))
    own = (iota(spread.shape, 1) & (CAP - 1)) == (iota(spread.shape, 0) & (CAP - 1))
    kind = iota((4 * CAP, 3 * LANES), 0) >> 4
    column = iota((4 * CAP, 3 * LANES), 1)
    fold = onehot(
        ((column < LANES) & (kind == 0))
        | ((column >= LANES) & (column < 2 * LANES) & (kind == 1))
        | ((column == 2 * LANES + 88) & (kind == 2))
        | ((column == 2 * LANES + 89) & (kind == 3))
        | ((column == 2 * LANES + 90) & (kind == 1))
    )
    known = dot(jnp.where(own, spread, 0.0).astype(bf16), fold)
    span_scr[...] = known[:, :LANES]
    seq_scr[...] = known[:, LANES : 2 * LANES]
    meta_scr[...] = known[:, 2 * LANES :]


def pack_rows(score_scr, turned_scr, levels, span_scr, seq_scr, meta_scr, out_ref):
    weights = score_scr[...]
    turned_scr[...] = jnp.concatenate([weights, weights], axis=0).T
    low = iota((SPANS, LANES), 1) < 64
    parts = [
        jnp.where(low, turned_scr[pl.ds(t, SPANS, stride=SPAN), :], turned_scr[pl.ds(t + 1, SPANS, stride=SPAN), :])
        for t in range(0, SPAN, 2)
    ]
    by_span = jnp.concatenate(parts, axis=1).astype(bf16)
    width = by_span.shape[1]
    source = iota((width, LANES), 0)
    target = iota((width, LANES), 1)
    fold = onehot((target < 64) & ((source >> 6) == (target >> 3)) & ((source & 7) == (target & 7)))
    first, second, third = pieces_of(levels)
    own = jnp.concatenate([first, second, third], axis=0)
    gap = jnp.zeros((8, LANES), f32)
    table = jnp.concatenate([gap] * 8 + [own, gap, pltpu.roll(own, 8, 1), gap], axis=0).astype(bf16)
    block = 128
    lane = iota((block, LANES), 1)
    lane_seq = ((lane & 63) >> 3).astype(f32) + 1.0
    rank = iota((block, LANES), 0) & (CAP - 1)
    for start in range(0, ROWS, block):
        span = span_scr[start : start + block, :]
        seq = seq_scr[start : start + block, :]
        pick = jnp.concatenate([onehot(lane.astype(f32) == span), onehot((lane + LANES).astype(f32) == span)], axis=1)
        found = dot(pick, by_span)
        mine = seq == lane_seq
        kept = [jnp.where(mine, found[:, i : i + LANES], 0.0) for i in range(0, width, LANES)]
        chooser = onehot(((lane < 8) & (seq == (lane + 1).astype(f32))) | ((lane >= 8) & (lane < 16) & (rank == lane - 8)))
        packed = dot(jnp.concatenate(kept, axis=1).astype(bf16), fold) + dot_nt(chooser, table)
        out_ref[start : start + block, :] = (packed + meta_scr[start : start + block, :]).astype(bf16)


def holder_kernel(
    pos_hbm, query_hbm, latent_hbm, key_up_hbm, chosen_hbm, slot_hbm, row_hbm, column_hbm, out_ref,
    pos_ref, query_ref, latent_ref, key_up_ref, chosen_ref, slot_ref, row_ref, column_ref, sems,
    angle_scr, q_scr, q_out, up_scr, cos_scr, sin_scr, slot_scr, span_scr, seq_scr, meta_scr, mask_scr, score_scr, turned_scr,
):
    small = [
        pltpu.make_async_copy(source, target, sems.at[i])
        for i, (source, target) in enumerate(
            [
                (chosen_hbm, chosen_ref),
                (slot_hbm, slot_ref),
                (pos_hbm, pos_ref),
                (row_hbm, row_ref),
                (column_hbm, column_ref),
                (query_hbm, query_ref),
                (key_up_hbm, key_up_ref),
            ]
        )
    ]
    for copy in small:
        copy.start()
    latents = [pltpu.make_async_copy(latent_hbm.at[s], latent_ref.at[s], sems.at[len(small) + s]) for s in range(SEQS)]
    for copy in latents:
        copy.start()
    for copy in small:
        copy.wait()
    pool = lax.axis_index("pool")
    plan(pool, chosen_ref, slot_ref, slot_scr, span_scr, seq_scr, meta_scr, mask_scr)
    rotate_queries(pos_ref, query_ref, row_ref, angle_scr, q_scr, q_out)
    key_angles(pool, column_ref, cos_scr, sin_scr)
    up_scr[...] = key_up_ref[...].astype(f32).T.astype(bf16)
    for copy in latents:
        copy.wait()
    levels = score_all(latents, latent_ref, up_scr, q_out, cos_scr, sin_scr, mask_scr, score_scr)
    pack_rows(score_scr, turned_scr, levels, span_scr, seq_scr, meta_scr, out_ref)


def score_all(latents, latent_ref, up_scr, q_out, cos_scr, sin_scr, mask_scr, score_scr):
    up = up_scr[...]
    cosine, sine = cos_scr[...], sin_scr[...]
    lane = iota((HEADS, LANES), 1)
    levels = jnp.zeros((HEADS, LANES), f32)
    for s in range(SEQS):
        keys = dot(up, latent_ref[s])
        a, b = keys[:HALF], keys[HALF:]
        turned = jnp.concatenate([a * cosine - b * sine, b * cosine + a * sine], axis=0).astype(bf16)
        scores = dot(q_out[s].astype(bf16), turned) * (1.0 / math.sqrt(HD))
        live = jnp.concatenate([mask_scr[2 * s : 2 * s + 1, :], mask_scr[2 * s + 1 : 2 * s + 2, :]], axis=1) > 0.5
        peak = jnp.max(jnp.where(live, scores, BIG_NEG), axis=1, keepdims=True)
        weights = jnp.where(live, jnp.exp(scores - peak), 0.0)
        total = jnp.sum(weights, axis=1, keepdims=True)
        some = total > 0.0
        safe = jnp.where(some, total, 1.0)
        score_scr[s * HEADS : (s + 1) * HEADS, :] = weights * (1.0 / safe)
        levels = jnp.where(lane == s, jnp.where(some, peak + jnp.log(safe), BIG_NEG), levels)
    return levels


def owner_kernel(packed_ref, values_ref, out_ref, slot_vec, slot_sca, sem, found_scr, sum_scr):
    packed = packed_ref[...].astype(f32).T
    slot_vec[...] = (packed[88:89] * 64.0 + packed[89:90]).astype(jnp.int32)
    copy = pltpu.make_async_copy(slot_vec, slot_sca, sem)
    copy.start()
    seq = packed[90:91]
    live = seq > 0.5
    mine = [seq == float(s + 1) for s in range(SEQS)]
    level = packed[64:72] + packed[72:80] + packed[80:88]
    every = packed[96:104] + packed[104:112] + packed[112:120]
    rank = iota((1, ROWS), 1) & (CAP - 1)
    level_of = jnp.zeros_like(level)
    for s in range(SEQS):
        here = rank == s
        top = jnp.max(jnp.where(here, every, BIG_NEG), axis=1, keepdims=True)
        total = jnp.sum(jnp.where(here, jnp.exp(every - top), 0.0), axis=1, keepdims=True)
        level_of = jnp.where(mine[s], top + jnp.log(total), level_of)
    factor = jnp.where(live, jnp.exp(level - level_of), 0.0)
    weights = [packed[t * HEADS : (t + 1) * HEADS] * factor for t in range(SPAN)]
    copy.wait()

    @pl.loop(0, ROWS // 16)
    def _(step):
        for i in range(16):
            row = step * 16 + i
            found_scr[pl.ds(pl.multiple_of(row * SPAN, SPAN), SPAN), :] = values_ref[slot_sca[0, row]].astype(f32)

    summed = jnp.zeros((SEQS * HEADS, HD), f32)
    for t in range(SPAN):
        left = jnp.concatenate([jnp.where(mine[s], weights[t], 0.0) for s in range(SEQS)], axis=0).astype(bf16)
        right = found_scr[pl.ds(t, ROWS, stride=SPAN), :].astype(bf16)
        summed = summed + dot(left, right)
    sum_scr[...] = summed
    result = jnp.concatenate([sum_scr[pl.ds(h, SEQS, stride=HEADS), :] for h in range(HEADS)], axis=1).astype(bf16)
    for p in range(POOLS):
        out_ref[p] = result


def combine_kernel(gathered_ref, weight_ref, out_ref):
    total = gathered_ref[0].astype(f32)
    for p in range(1, POOLS):
        total = total + gathered_ref[p].astype(f32)
    projected = dot(total.astype(bf16), weight_ref[...])
    groups = out_ref.shape[0]
    width = projected.shape[1] // groups
    for g in range(groups):
        at = g * width
        half = projected[:, at // LANES * LANES : (at // LANES + 1) * LANES]
        out_ref[g] = pltpu.roll(half, (LANES - at % LANES) % LANES, 1)


def finish_kernel(parts_ref, out_ref):
    total = parts_ref[0]
    for g in range(1, parts_ref.shape[0]):
        total = total + parts_ref[g]
    out_ref[...] = total[:, : out_ref.shape[1]].astype(bf16)


def score(*operands):
    buffers = [pltpu.SMEM(operands[0].shape, jnp.int32)]
    buffers += [pltpu.VMEM(x.shape, x.dtype) for x in operands[1:]]
    return pl.pallas_call(
        holder_kernel,
        in_specs=[pl.BlockSpec(memory_space=pltpu.HBM)] * len(operands),
        out_specs=pl.BlockSpec(memory_space=pltpu.VMEM),
        out_shape=jax.ShapeDtypeStruct((ROWS, LANES), bf16),
        scratch_shapes=[
            *buffers,
            pltpu.SemaphoreType.DMA((len(operands) - 1 + SEQS,)),
            pltpu.VMEM((3, SEQS, LANES), f32),
            pltpu.VMEM((SEQS * HEADS, HD), f32),
            pltpu.VMEM((SEQS, HEADS, HD), f32),
            pltpu.VMEM((HD, RANK), bf16),
            pltpu.VMEM((HALF, TOKENS), f32),
            pltpu.VMEM((HALF, TOKENS), f32),
            pltpu.VMEM((CHUNKS, LANES), jnp.int32),
            pltpu.VMEM((ROWS, LANES), f32),
            pltpu.VMEM((ROWS, LANES), f32),
            pltpu.VMEM((ROWS, LANES), f32),
            pltpu.VMEM((CHUNKS, LANES * SPAN), f32),
            pltpu.VMEM((SEQS * HEADS, TOKENS), f32),
            pltpu.VMEM((TOKENS, LANES), f32),
        ],
        compiler_params=pltpu.CompilerParams(vmem_limit_bytes=32 << 20),
        name="score",
    )(*[pltpu.with_memory_space_constraint(x, pltpu.HBM) for x in operands])


def weigh(packed, values):
    return pl.pallas_call(
        owner_kernel,
        in_specs=[pl.BlockSpec(memory_space=pltpu.VMEM)] * 2,
        out_specs=pl.BlockSpec(memory_space=pltpu.VMEM),
        out_shape=jax.ShapeDtypeStruct((POOLS, SEQS, HEADS * HD), bf16),
        scratch_shapes=[
            pltpu.VMEM((1, ROWS), jnp.int32),
            pltpu.SMEM((1, ROWS), jnp.int32),
            pltpu.SemaphoreType.DMA,
            pltpu.VMEM((ROWS * SPAN, HD), f32),
            pltpu.VMEM((SEQS * HEADS, HD), f32),
        ],
        compiler_params=pltpu.CompilerParams(vmem_limit_bytes=24 << 20),
        name="weigh",
    )(packed, values)


def combine(gathered, out_weight, groups):
    return pl.pallas_call(
        combine_kernel,
        in_specs=[pl.BlockSpec(memory_space=pltpu.VMEM)] * 2,
        out_specs=pl.BlockSpec(memory_space=pltpu.VMEM),
        out_shape=jax.ShapeDtypeStruct((groups, SEQS, LANES), f32),
        compiler_params=pltpu.CompilerParams(vmem_limit_bytes=16 << 20),
        name="combine",
    )(gathered, out_weight)


def finish(parts, width):
    return pl.pallas_call(
        finish_kernel,
        in_specs=[pl.BlockSpec(memory_space=pltpu.VMEM)],
        out_specs=pl.BlockSpec(memory_space=pltpu.VMEM),
        out_shape=jax.ShapeDtypeStruct((SEQS, width), bf16),
        compiler_params=pltpu.CompilerParams(vmem_limit_bytes=8 << 20),
        name="finish",
    )(parts)


def on_device(query, query_pos, key_latent, key_up, value_cache, chosen, value_slot, out_weight):
    row_table, column_table = angle_tables()
    latent = jnp.swapaxes(key_latent, 1, 2)
    slot_rows = value_slot.reshape(-1, LANES)
    packed = score(query_pos, query, latent, key_up, chosen, slot_rows, row_table, column_table)
    arrived = lax.all_to_all(packed.reshape(POOLS, CAP, LANES), "pool", split_axis=0, concat_axis=0, tiled=True)
    partial = weigh(arrived.reshape(ROWS, LANES), value_cache)
    gathered = lax.all_to_all(partial, "pool", split_axis=0, concat_axis=0, tiled=True)
    groups = lax.axis_size("head")
    projected = combine(gathered, out_weight, groups)
    parts = lax.all_to_all(projected, "head", split_axis=0, concat_axis=0, tiled=True)
    return finish(parts, out_weight.shape[1] // groups)


def solution(mesh):
    placed = (
        P(None, "head"),
        P(),
        P(None, "pool", None),
        P(None, "head"),
        P("pool", None, "head"),
        P(),
        P(),
        P("head", "pool"),
    )
    return jax.shard_map(
        on_device, mesh=mesh, in_specs=placed, out_specs=P(None, ("pool", "head")), check_vma=False
    )
```

```python
import math

import jax
import jax.numpy as jnp
import numpy as np
from jax import lax
from jax.experimental import pallas as pl
from jax.experimental.pallas import tpu as pltpu
from jax.sharding import Mesh
from jax.sharding import PartitionSpec as P

SEQS = 8
HEADS = 8
HD = 128
HALF = HD // 2
RANK = 160
SPAN = 8
THETA = 500000.0
LANES = 128

POOLS = 32
PAIRS = POOLS // 2
CAP = 16
ROWS = POOLS * CAP
SPANS = 256
TOKENS = SPANS * SPAN
SLOTS = 2048
CHUNKS = SEQS * SPANS // LANES
BIG_NEG = -1e30

f32 = jnp.float32
bf16 = jnp.bfloat16

HI_ROWS, MID_ROWS, LO_ROWS = 40, 16, 128
MID_AT, LO_AT = HI_ROWS, HI_ROWS + MID_ROWS


def angle_tables():
    inverse = np.exp(-(2.0 * np.arange(HALF) / HD) * math.log(THETA))
    rows = np.concatenate([np.arange(HI_ROWS) * 2048.0, np.arange(MID_ROWS) * 128.0, np.arange(LO_ROWS) * 1.0])
    angles = rows[:, None] * inverse[None, :]
    row_table = np.concatenate([np.cos(angles), np.sin(angles)], axis=1).astype(np.float32)
    lanes = np.arange(LANES)
    columns = np.concatenate([np.minimum(lanes, HI_ROWS - 1) * 2048.0, np.minimum(lanes, MID_ROWS - 1) * 128.0, lanes * 1.0])
    angles = inverse[:, None] * columns[None, :]
    column_table = np.concatenate([np.cos(angles), np.sin(angles)], axis=0).astype(np.float32)
    return row_table, column_table


def iota(shape, dim):
    return lax.broadcasted_iota(jnp.int32, shape, dim)


def onehot(condition):
    return jnp.where(condition, 1.0, 0.0).astype(bf16)


def dot(a, b):
    return lax.dot_general(a, b, (((1,), (0,)), ((), ())), preferred_element_type=f32)


def dot_nt(a, b):
    return lax.dot_general(a, b, (((1,), (1,)), ((), ())), preferred_element_type=f32)


def pieces_of(x):
    first = x.astype(bf16).astype(f32)
    rest = x - first
    second = rest.astype(bf16).astype(f32)
    return first, second, rest - second


def rotate_queries(pos_ref, query_ref, row_ref, angle_scr, q_scr, q_out):
    for s in range(SEQS):
        pos = pos_ref[s]
        angle_scr[0, s : s + 1, :] = row_ref[pl.ds(pos >> 11, 1), :]
        angle_scr[1, s : s + 1, :] = row_ref[pl.ds(MID_AT + ((pos >> 7) & 15), 1), :]
        angle_scr[2, s : s + 1, :] = row_ref[pl.ds(LO_AT + (pos & 127), 1), :]
    first, second, third = angle_scr[0], angle_scr[1], angle_scr[2]
    cosine = first[:, :HALF] * second[:, :HALF] - first[:, HALF:] * second[:, HALF:]
    sine = first[:, HALF:] * second[:, :HALF] + first[:, :HALF] * second[:, HALF:]
    cosine, sine = (
        cosine * third[:, :HALF] - sine * third[:, HALF:],
        sine * third[:, :HALF] + cosine * third[:, HALF:],
    )
    for h in range(HEADS):
        rows = query_ref[:, h * HD : (h + 1) * HD].astype(f32)
        a, b = rows[:, :HALF], rows[:, HALF:]
        turned = jnp.concatenate([a * cosine - b * sine, b * cosine + a * sine], axis=1)
        q_scr[h * SEQS : (h + 1) * SEQS, :] = turned.astype(bf16).astype(f32)
    for s in range(SEQS):
        q_out[s] = q_scr[pl.ds(s, HEADS, stride=SEQS), :]


def key_angles(pool, column_ref, cos_scr, sin_scr):
    lane = iota((HD, LANES), 1)
    base = jnp.sum(jnp.where(lane == pool, column_ref[:, :LANES], 0.0), axis=1, keepdims=True)
    cp, sp = base[:HALF], base[HALF:]
    c2, s2 = column_ref[:HALF, LANES : 2 * LANES], column_ref[HALF:, LANES : 2 * LANES]
    cb, sb = cp * c2 - sp * s2, sp * c2 + cp * s2
    c3, s3 = column_ref[:HALF, 2 * LANES :], column_ref[HALF:, 2 * LANES :]
    for c in range(TOKENS // LANES):
        ca, sa = cb[:, c : c + 1], sb[:, c : c + 1]
        cos_scr[:, c * LANES : (c + 1) * LANES] = ca * c3 - sa * s3
        sin_scr[:, c * LANES : (c + 1) * LANES] = sa * c3 + ca * s3


def plan(pool, chosen_ref, slot_ref, slot_scr, span_scr, seq_scr, meta_scr, mask_scr):
    relative = chosen_ref[...] - pool * SPANS
    here = (relative >= 0) & (relative < SPANS)
    row_code = jnp.where(here, 2 * iota(relative.shape, 0) + (relative >> 7), -1)
    lane_code = relative & 127
    picks = relative.shape[1]
    left = [onehot(iota((CHUNKS, picks), 0) == row_code[s : s + 1, :]) for s in range(SEQS)]
    right = [onehot(iota((LANES, picks), 0) == lane_code[s : s + 1, :]) for s in range(SEQS)]
    member = dot_nt(jnp.concatenate(left, axis=1), jnp.concatenate(right, axis=1))
    mask_scr[...] = dot(member.astype(bf16), onehot(iota((LANES, LANES * SPAN), 0) == (iota((LANES, LANES * SPAN), 1) >> 3)))
    for s in range(SEQS):
        slot_scr[2 * s : 2 * s + 2, :] = slot_ref[pl.ds(s * (SPANS * POOLS // LANES) + 2 * pool, 2), :]
    slots = slot_scr[...]
    owner = jnp.where(member > 0.5, slots >> 11, -1)
    local_slot = slots & (SLOTS - 1)
    owners = [jnp.where(iota((POOLS, LANES), 0) == owner[c : c + 1, :], 1.0, 0.0) for c in range(CHUNKS)]
    earlier = iota((LANES, 2 * LANES), 0) < iota((LANES, 2 * LANES), 1)
    counted = dot(jnp.concatenate(owners, axis=0).astype(bf16), onehot(earlier))
    carry = jnp.zeros((POOLS, LANES), f32)
    facts = []
    for c in range(CHUNKS):
        part = counted[c * POOLS : (c + 1) * POOLS]
        rank = jnp.sum(owners[c] * (part[:, :LANES] + carry), axis=0, keepdims=True).astype(jnp.int32)
        carry = carry + part[:, LANES:]
        at_rank = jnp.where(iota((CAP, LANES), 0) == rank, 1.0, 0.0)
        span = (iota((1, LANES), 1) + (c % 2) * LANES).astype(f32)
        slot = local_slot[c : c + 1, :]
        facts.append(
            jnp.concatenate(
                [
                    at_rank * span,
                    at_rank * float(c // 2 + 1),
                    at_rank * (slot >> 6).astype(f32),
                    at_rank * (slot & 63).astype(f32),
                ],
                axis=0,
            )
        )
    table = dot_nt(
        jnp.concatenate(owners, axis=1).astype(bf16), jnp.concatenate(facts, axis=1).astype(bf16)
    )
    spread = dot(onehot((iota((ROWS, POOLS), 0) >> 4) == iota((ROWS, POOLS), 1)), table.astype(bf16))
    own = (iota(spread.shape, 1) & (CAP - 1)) == (iota(spread.shape, 0) & (CAP - 1))
    kind = iota((4 * CAP, 3 * LANES), 0) >> 4
    column = iota((4 * CAP, 3 * LANES), 1)
    fold = onehot(
        ((column < LANES) & (kind == 0))
        | ((column >= LANES) & (column < 2 * LANES) & (kind == 1))
        | ((column == 2 * LANES + 88) & (kind == 2))
        | ((column == 2 * LANES + 89) & (kind == 3))
        | ((column == 2 * LANES + 90) & (kind == 1))
    )
    known = dot(jnp.where(own, spread, 0.0).astype(bf16), fold)
    span_scr[...] = known[:, :LANES]
    seq_scr[...] = known[:, LANES : 2 * LANES]
    meta_scr[...] = known[:, 2 * LANES :]


def pack_rows(score_scr, turned_scr, levels, span_scr, seq_scr, meta_scr, out_ref):
    weights = score_scr[...]
    turned_scr[...] = jnp.concatenate([weights, weights], axis=0).T
    low = iota((SPANS, LANES), 1) < 64
    parts = [
        jnp.where(low, turned_scr[pl.ds(t, SPANS, stride=SPAN), :], turned_scr[pl.ds(t + 1, SPANS, stride=SPAN), :])
        for t in range(0, SPAN, 2)
    ]
    by_span = jnp.concatenate(parts, axis=1).astype(bf16)
    width = by_span.shape[1]
    source = iota((width, LANES), 0)
    target = iota((width, LANES), 1)
    fold = onehot((target < 64) & ((source >> 6) == (target >> 3)) & ((source & 7) == (target & 7)))
    first, second, third = pieces_of(levels)
    own = jnp.concatenate([first, second, third], axis=0)
    gap = jnp.zeros((8, LANES), f32)
    table = jnp.concatenate([gap] * 8 + [own, gap, pltpu.roll(own, 8, 1), gap], axis=0)
    fold = jnp.concatenate([fold, table.T.astype(bf16)], axis=0)
    lane = iota((ROWS, LANES), 1)
    lane_seq = ((lane & 63) >> 3).astype(f32) + 1.0
    rank = iota((ROWS, LANES), 0) & (CAP - 1)
    span = span_scr[...]
    seq = seq_scr[...]
    pick = jnp.concatenate([onehot(lane.astype(f32) == span), onehot((lane + LANES).astype(f32) == span)], axis=1)
    chooser = onehot(((lane < 8) & (seq == (lane + 1).astype(f32))) | ((lane >= 8) & (lane < 16) & (rank == lane - 8)))
    found = dot(pick, by_span)
    mine = seq == lane_seq
    kept = [jnp.where(mine, found[:, i : i + LANES], 0.0).astype(bf16) for i in range(0, width, LANES)]
    packed = dot(jnp.concatenate(kept + [chooser], axis=1), fold)
    out_ref[...] = (packed + meta_scr[...]).astype(bf16)


def holder_kernel(
    pos_hbm, query_hbm, latent_hbm, key_up_hbm, chosen_hbm, slot_hbm, row_hbm, column_hbm, out_ref,
    pos_ref, query_ref, latent_ref, key_up_ref, chosen_ref, slot_ref, row_ref, column_ref, sems,
    angle_scr, q_scr, q_out, up_scr, cos_scr, sin_scr, slot_scr, span_scr, seq_scr, meta_scr, mask_scr, score_scr, turned_scr, turned_keys,
):
    small = [
        pltpu.make_async_copy(source, target, sems.at[i])
        for i, (source, target) in enumerate(
            [
                (chosen_hbm, chosen_ref),
                (slot_hbm, slot_ref),
                (pos_hbm, pos_ref),
                (row_hbm, row_ref),
                (column_hbm, column_ref),
                (query_hbm, query_ref),
                (key_up_hbm, key_up_ref),
            ]
        )
    ]
    for copy in small:
        copy.start()
    latents = [pltpu.make_async_copy(latent_hbm.at[s], latent_ref.at[s], sems.at[len(small) + s]) for s in range(SEQS)]
    for copy in latents:
        copy.start()
    for copy in small:
        copy.wait()
    pool = lax.axis_index("pair") * 2 + lax.axis_index("side")
    plan(pool, chosen_ref, slot_ref, slot_scr, span_scr, seq_scr, meta_scr, mask_scr)
    rotate_queries(pos_ref, query_ref, row_ref, angle_scr, q_scr, q_out)
    key_angles(pool, column_ref, cos_scr, sin_scr)
    up_scr[...] = key_up_ref[...].astype(f32).T.astype(bf16)
    for copy in latents:
        copy.wait()
    levels = score_all(turned_keys, latent_ref, up_scr, q_out, cos_scr, sin_scr, mask_scr, score_scr)
    pack_rows(score_scr, turned_scr, levels, span_scr, seq_scr, meta_scr, out_ref)


def score_all(turned_keys, latent_ref, up_scr, q_out, cos_scr, sin_scr, mask_scr, score_scr):
    up = up_scr[...]
    cosine, sine = cos_scr[...], sin_scr[...]
    lane = iota((HEADS, LANES), 1)
    levels = jnp.zeros((HEADS, LANES), f32)
    for s in range(SEQS):
        for at in range(0, TOKENS, 256):
            keys = dot(up, latent_ref[s, :, at : at + 256])
            a, b = keys[:HALF], keys[HALF:]
            co, si = cos_scr[:, at : at + 256], sin_scr[:, at : at + 256]
            turned_keys[s * HD : s * HD + HALF, at : at + 256] = (a * co - b * si).astype(bf16)
            turned_keys[s * HD + HALF : (s + 1) * HD, at : at + 256] = (b * co + a * si).astype(bf16)
    gap = jnp.zeros((HEADS, HD), f32)
    spread = [jnp.concatenate([q_out[s] if i == s else gap for i in range(SEQS)], axis=1) for s in range(SEQS)]
    every = dot(jnp.concatenate(spread, axis=0).astype(bf16), turned_keys[...]) * (1.0 / math.sqrt(HD))
    for s in range(SEQS):
        scores = every[s * HEADS : (s + 1) * HEADS]
        live = jnp.concatenate([mask_scr[2 * s : 2 * s + 1, :], mask_scr[2 * s + 1 : 2 * s + 2, :]], axis=1) > 0.5
        peak = jnp.max(jnp.where(live, scores, BIG_NEG), axis=1, keepdims=True)
        weights = jnp.where(live, jnp.exp(scores - peak), 0.0)
        total = jnp.sum(weights, axis=1, keepdims=True)
        some = total > 0.0
        safe = jnp.where(some, total, 1.0)
        score_scr[s * HEADS : (s + 1) * HEADS, :] = weights * (1.0 / safe)
        levels = jnp.where(lane == s, jnp.where(some, peak + jnp.log(safe), BIG_NEG), levels)
    return levels


def owner_kernel(packed_ref, values_ref, out_ref, slot_vec, slot_sca, sem, found_scr, sum_scr):
    packed = packed_ref[...].astype(f32).T
    slot_vec[...] = (packed[88:89] * 64.0 + packed[89:90]).astype(jnp.int32)
    copy = pltpu.make_async_copy(slot_vec, slot_sca, sem)
    copy.start()
    seq = packed[90:91]
    live = seq > 0.5
    mine = [seq == float(s + 1) for s in range(SEQS)]
    level = packed[64:72] + packed[72:80] + packed[80:88]
    every = packed[96:104] + packed[104:112] + packed[112:120]
    rank = iota((1, ROWS), 1) & (CAP - 1)
    level_of = jnp.zeros_like(level)
    for s in range(SEQS):
        here = rank == s
        top = jnp.max(jnp.where(here, every, BIG_NEG), axis=1, keepdims=True)
        total = jnp.sum(jnp.where(here, jnp.exp(every - top), 0.0), axis=1, keepdims=True)
        level_of = jnp.where(mine[s], top + jnp.log(total), level_of)
    factor = jnp.where(live, jnp.exp(level - level_of), 0.0)
    weights = [packed[t * HEADS : (t + 1) * HEADS] * factor for t in range(SPAN)]
    copy.wait()

    @pl.loop(0, ROWS // 16)
    def _(step):
        for i in range(16):
            row = step * 16 + i
            found_scr[pl.ds(pl.multiple_of(row * SPAN, SPAN), SPAN), :] = values_ref[slot_sca[0, row]].astype(f32)

    left = [jnp.concatenate([jnp.where(mine[s], weights[t], 0.0) for s in range(SEQS)], axis=0).astype(bf16) for t in range(SPAN)]
    right = [found_scr[pl.ds(t, ROWS, stride=SPAN), :].astype(bf16) for t in range(SPAN)]
    sum_scr[...] = dot(jnp.concatenate(left, axis=1), jnp.concatenate(right, axis=0))
    result = jnp.concatenate([sum_scr[pl.ds(h, SEQS, stride=HEADS), :] for h in range(HEADS)], axis=1).astype(bf16)
    for p in range(PAIRS):
        out_ref[p] = result


def combine_kernel(gathered_ref, *refs):
    *weight_refs, out_ref = refs
    total = gathered_ref[0].astype(f32)
    for p in range(1, PAIRS):
        total = total + gathered_ref[p].astype(f32)
    total = total.astype(bf16)
    side = lax.axis_index("side")
    groups = out_ref.shape[0] // 2
    for k in range(2):
        projected = dot(total, weight_refs[k][...])
        width = projected.shape[1] // groups
        for g in range(groups):
            at = g * width
            half = projected[:, at // LANES * LANES : (at // LANES + 1) * LANES]
            out_ref[(side ^ k) * groups + g] = pltpu.roll(half, (LANES - at % LANES) % LANES, 1)


def finish_kernel(parts_ref, out_ref):
    total = parts_ref[0]
    for g in range(1, parts_ref.shape[0]):
        total = total + parts_ref[g]
    out_ref[...] = total[:, : out_ref.shape[1]].astype(bf16)


def score(*operands):
    buffers = [pltpu.SMEM(operands[0].shape, jnp.int32)]
    buffers += [pltpu.VMEM(x.shape, x.dtype) for x in operands[1:]]
    return pl.pallas_call(
        holder_kernel,
        in_specs=[pl.BlockSpec(memory_space=pltpu.HBM)] * len(operands),
        out_specs=pl.BlockSpec(memory_space=pltpu.VMEM),
        out_shape=jax.ShapeDtypeStruct((ROWS, LANES), bf16),
        scratch_shapes=[
            *buffers,
            pltpu.SemaphoreType.DMA((len(operands) - 1 + SEQS,)),
            pltpu.VMEM((3, SEQS, LANES), f32),
            pltpu.VMEM((SEQS * HEADS, HD), f32),
            pltpu.VMEM((SEQS, HEADS, HD), f32),
            pltpu.VMEM((HD, RANK), bf16),
            pltpu.VMEM((HALF, TOKENS), f32),
            pltpu.VMEM((HALF, TOKENS), f32),
            pltpu.VMEM((CHUNKS, LANES), jnp.int32),
            pltpu.VMEM((ROWS, LANES), f32),
            pltpu.VMEM((ROWS, LANES), f32),
            pltpu.VMEM((ROWS, LANES), f32),
            pltpu.VMEM((CHUNKS, LANES * SPAN), f32),
            pltpu.VMEM((SEQS * HEADS, TOKENS), f32),
            pltpu.VMEM((TOKENS, LANES), f32),
            pltpu.VMEM((SEQS * HD, TOKENS), bf16),
        ],
        compiler_params=pltpu.CompilerParams(vmem_limit_bytes=32 << 20),
        name="score",
    )(*[pltpu.with_memory_space_constraint(x, pltpu.HBM) for x in operands])


def weigh(packed, values):
    return pl.pallas_call(
        owner_kernel,
        in_specs=[pl.BlockSpec(memory_space=pltpu.VMEM)] * 2,
        out_specs=pl.BlockSpec(memory_space=pltpu.VMEM),
        out_shape=jax.ShapeDtypeStruct((PAIRS, SEQS, HEADS * HD), bf16),
        scratch_shapes=[
            pltpu.VMEM((1, ROWS), jnp.int32),
            pltpu.SMEM((1, ROWS), jnp.int32),
            pltpu.SemaphoreType.DMA,
            pltpu.VMEM((ROWS * SPAN, HD), f32),
            pltpu.VMEM((SEQS * HEADS, HD), f32),
        ],
        compiler_params=pltpu.CompilerParams(vmem_limit_bytes=24 << 20),
        name="weigh",
    )(packed, values)


def combine(gathered, weights, groups):
    return pl.pallas_call(
        combine_kernel,
        in_specs=[pl.BlockSpec(memory_space=pltpu.VMEM)] * 3,
        out_specs=pl.BlockSpec(memory_space=pltpu.VMEM),
        out_shape=jax.ShapeDtypeStruct((2 * groups, SEQS, LANES), f32),
        compiler_params=pltpu.CompilerParams(vmem_limit_bytes=16 << 20),
        name="combine",
    )(gathered, *weights)


def finish(parts, width):
    return pl.pallas_call(
        finish_kernel,
        in_specs=[pl.BlockSpec(memory_space=pltpu.VMEM)],
        out_specs=pl.BlockSpec(memory_space=pltpu.VMEM),
        out_shape=jax.ShapeDtypeStruct((SEQS, width), bf16),
        compiler_params=pltpu.CompilerParams(vmem_limit_bytes=8 << 20),
        name="finish",
    )(parts)


def on_device(query, query_pos, key_latent, key_up, value_cache, chosen, value_slot, out_weight):
    row_table, column_table = angle_tables()
    latent = jnp.swapaxes(key_latent, 1, 2)
    slot_rows = value_slot.reshape(-1, LANES)
    weights = [out_weight, lax.ppermute(out_weight, "side", [(0, 1), (1, 0)])]
    packed = score(query_pos, query, latent, key_up, chosen, slot_rows, row_table, column_table)
    arrived = lax.all_to_all(packed.reshape(POOLS, CAP, LANES), ("pair", "side"), split_axis=0, concat_axis=0, tiled=True)
    arrived, weights[1] = lax.optimization_barrier((arrived, weights[1]))
    partial = weigh(arrived.reshape(ROWS, LANES), value_cache)
    gathered = lax.all_to_all(partial, "pair", split_axis=0, concat_axis=0, tiled=True)
    groups = lax.axis_size("head")
    projected = combine(gathered, weights, groups)
    parts = lax.all_to_all(projected, ("side", "head"), split_axis=0, concat_axis=0, tiled=True)
    return finish(parts, out_weight.shape[1] // groups)


def solution(mesh):
    split = Mesh(mesh.devices.reshape(PAIRS, 2, -1), ("pair", "side", "head"))
    placed = (
        P(None, "head"),
        P(),
        P(None, ("pair", "side"), None),
        P(None, "head"),
        P(("pair", "side"), None, "head"),
        P(),
        P(),
        P("head", ("pair", "side")),
    )
    return jax.shard_map(
        on_device, mesh=split, in_specs=placed, out_specs=P(None, ("pair", "side", "head")), check_vma=False
    )
```

```python
import math

import jax
import jax.numpy as jnp
import numpy as np
from jax import lax
from jax.experimental import pallas as pl
from jax.experimental.pallas import tpu as pltpu
from jax.sharding import Mesh
from jax.sharding import PartitionSpec as P

SEQS = 8
HEADS = 8
HD = 128
HALF = HD // 2
RANK = 160
SPAN = 8
THETA = 500000.0
LANES = 128

POOLS = 32
PAIRS = POOLS // 2
CAP = 16
ROWS = POOLS * CAP
SPANS = 256
TOKENS = SPANS * SPAN
SLOTS = 2048
CHUNKS = SEQS * SPANS // LANES
BIG_NEG = -1e30
BATCH = 512

f32 = jnp.float32
bf16 = jnp.bfloat16

HI_ROWS, MID_ROWS, LO_ROWS = 40, 16, 128
MID_AT, LO_AT = HI_ROWS, HI_ROWS + MID_ROWS


def angle_tables():
    inverse = np.exp(-(2.0 * np.arange(HALF) / HD) * math.log(THETA))
    rows = np.concatenate([np.arange(HI_ROWS) * 2048.0, np.arange(MID_ROWS) * 128.0, np.arange(LO_ROWS) * 1.0])
    angles = rows[:, None] * inverse[None, :]
    row_table = np.concatenate([np.cos(angles), np.sin(angles)], axis=1).astype(np.float32)
    lanes = np.arange(LANES)
    columns = np.concatenate([np.minimum(lanes, HI_ROWS - 1) * 2048.0, np.minimum(lanes, MID_ROWS - 1) * 128.0, lanes * 1.0])
    angles = inverse[:, None] * columns[None, :]
    column_table = np.concatenate([np.cos(angles), np.sin(angles)], axis=0).astype(np.float32)
    return row_table, column_table


def iota(shape, dim):
    return lax.broadcasted_iota(jnp.int32, shape, dim)


def onehot(condition):
    return jnp.where(condition, 1.0, 0.0).astype(bf16)


def dot(a, b):
    return lax.dot_general(a, b, (((1,), (0,)), ((), ())), preferred_element_type=f32)


def dot_nt(a, b):
    return lax.dot_general(a, b, (((1,), (1,)), ((), ())), preferred_element_type=f32)


def pieces_of(x):
    first = x.astype(bf16).astype(f32)
    rest = x - first
    second = rest.astype(bf16).astype(f32)
    return first, second, rest - second


def rotate_queries(pos_ref, query_ref, row_ref, angle_scr, q_scr, q_out):
    for s in range(SEQS):
        pos = pos_ref[s]
        angle_scr[0, s : s + 1, :] = row_ref[pl.ds(pos >> 11, 1), :]
        angle_scr[1, s : s + 1, :] = row_ref[pl.ds(MID_AT + ((pos >> 7) & 15), 1), :]
        angle_scr[2, s : s + 1, :] = row_ref[pl.ds(LO_AT + (pos & 127), 1), :]
    first, second, third = angle_scr[0], angle_scr[1], angle_scr[2]
    cosine = first[:, :HALF] * second[:, :HALF] - first[:, HALF:] * second[:, HALF:]
    sine = first[:, HALF:] * second[:, :HALF] + first[:, :HALF] * second[:, HALF:]
    cosine, sine = (
        cosine * third[:, :HALF] - sine * third[:, HALF:],
        sine * third[:, :HALF] + cosine * third[:, HALF:],
    )
    for h in range(HEADS):
        rows = query_ref[:, h * HD : (h + 1) * HD].astype(f32)
        a, b = rows[:, :HALF], rows[:, HALF:]
        turned = jnp.concatenate([a * cosine - b * sine, b * cosine + a * sine], axis=1)
        q_scr[h * SEQS : (h + 1) * SEQS, :] = turned.astype(bf16).astype(f32)
    for s in range(SEQS):
        q_out[s] = q_scr[pl.ds(s, HEADS, stride=SEQS), :]


def key_angles(pool, column_ref, cos_scr, sin_scr):
    lane = iota((HD, LANES), 1)
    base = jnp.sum(jnp.where(lane == pool, column_ref[:, :LANES], 0.0), axis=1, keepdims=True)
    cp, sp = base[:HALF], base[HALF:]
    c2, s2 = column_ref[:HALF, LANES : 2 * LANES], column_ref[HALF:, LANES : 2 * LANES]
    cb, sb = cp * c2 - sp * s2, sp * c2 + cp * s2
    c3, s3 = column_ref[:HALF, 2 * LANES :], column_ref[HALF:, 2 * LANES :]
    for c in range(TOKENS // LANES):
        ca, sa = cb[:, c : c + 1], sb[:, c : c + 1]
        cos_scr[:, c * LANES : (c + 1) * LANES] = ca * c3 - sa * s3
        sin_scr[:, c * LANES : (c + 1) * LANES] = sa * c3 + ca * s3


def plan(pool, chosen_ref, slot_ref, slot_scr, span_scr, seq_scr, meta_scr, mask_scr):
    relative = chosen_ref[...] - pool * SPANS
    here = (relative >= 0) & (relative < SPANS)
    row_code = jnp.where(here, 2 * iota(relative.shape, 0) + (relative >> 7), -1)
    lane_code = relative & 127
    picks = relative.shape[1]
    left = [onehot(iota((CHUNKS, picks), 0) == row_code[s : s + 1, :]) for s in range(SEQS)]
    right = [onehot(iota((LANES, picks), 0) == lane_code[s : s + 1, :]) for s in range(SEQS)]
    member = dot_nt(jnp.concatenate(left, axis=1), jnp.concatenate(right, axis=1))
    mask_scr[...] = dot(member.astype(bf16), onehot(iota((LANES, LANES * SPAN), 0) == (iota((LANES, LANES * SPAN), 1) >> 3)))
    for s in range(SEQS):
        slot_scr[2 * s : 2 * s + 2, :] = slot_ref[pl.ds(s * (SPANS * POOLS // LANES) + 2 * pool, 2), :]
    slots = slot_scr[...]
    owner = jnp.where(member > 0.5, slots >> 11, -1)
    local_slot = slots & (SLOTS - 1)
    owners = [jnp.where(iota((POOLS, LANES), 0) == owner[c : c + 1, :], 1.0, 0.0) for c in range(CHUNKS)]
    earlier = iota((LANES, 2 * LANES), 0) < iota((LANES, 2 * LANES), 1)
    counted = dot(jnp.concatenate(owners, axis=0).astype(bf16), onehot(earlier))
    carry = jnp.zeros((POOLS, LANES), f32)
    facts = []
    for c in range(CHUNKS):
        part = counted[c * POOLS : (c + 1) * POOLS]
        rank = jnp.sum(owners[c] * (part[:, :LANES] + carry), axis=0, keepdims=True).astype(jnp.int32)
        carry = carry + part[:, LANES:]
        at_rank = jnp.where(iota((CAP, LANES), 0) == rank, 1.0, 0.0)
        span = (iota((1, LANES), 1) + (c % 2) * LANES).astype(f32)
        slot = local_slot[c : c + 1, :]
        facts.append(
            jnp.concatenate(
                [
                    at_rank * span,
                    at_rank * float(c // 2 + 1),
                    at_rank * (slot >> 6).astype(f32),
                    at_rank * (slot & 63).astype(f32),
                ],
                axis=0,
            )
        )
    table = dot_nt(
        jnp.concatenate(owners, axis=1).astype(bf16), jnp.concatenate(facts, axis=1).astype(bf16)
    )
    spread = dot(onehot((iota((ROWS, POOLS), 0) >> 4) == iota((ROWS, POOLS), 1)), table.astype(bf16))
    own = (iota(spread.shape, 1) & (CAP - 1)) == (iota(spread.shape, 0) & (CAP - 1))
    kind = iota((4 * CAP, 3 * LANES), 0) >> 4
    column = iota((4 * CAP, 3 * LANES), 1)
    fold = onehot(
        ((column < LANES) & (kind == 0))
        | ((column >= LANES) & (column < 2 * LANES) & (kind == 1))
        | ((column == 2 * LANES + 88) & (kind == 2))
        | ((column == 2 * LANES + 89) & (kind == 3))
        | ((column == 2 * LANES + 90) & (kind == 1))
    )
    known = dot(jnp.where(own, spread, 0.0).astype(bf16), fold)
    span_scr[...] = known[:, :LANES]
    seq_scr[...] = known[:, LANES : 2 * LANES]
    meta_scr[...] = known[:, 2 * LANES :]


def pack_rows(score_scr, turned_scr, levels, span_scr, seq_scr, meta_scr, out_ref):
    weights = score_scr[...]
    turned_scr[...] = jnp.concatenate([weights, weights], axis=0).T
    low = iota((SPANS, LANES), 1) < 64
    parts = [
        jnp.where(low, turned_scr[pl.ds(t, SPANS, stride=SPAN), :], turned_scr[pl.ds(t + 1, SPANS, stride=SPAN), :])
        for t in range(0, SPAN, 2)
    ]
    by_span = jnp.concatenate(parts, axis=1).astype(bf16)
    width = by_span.shape[1]
    source = iota((width, LANES), 0)
    target = iota((width, LANES), 1)
    fold = onehot((target < 64) & ((source >> 6) == (target >> 3)) & ((source & 7) == (target & 7)))
    first, second, third = pieces_of(levels)
    own = jnp.concatenate([first, second, third], axis=0)
    gap = jnp.zeros((8, LANES), f32)
    table = jnp.concatenate([gap] * 8 + [own, gap, pltpu.roll(own, 8, 1), gap], axis=0)
    fold = jnp.concatenate([fold, table.T.astype(bf16)], axis=0)
    lane = iota((ROWS, LANES), 1)
    lane_seq = ((lane & 63) >> 3).astype(f32) + 1.0
    rank = iota((ROWS, LANES), 0) & (CAP - 1)
    span = span_scr[...]
    seq = seq_scr[...]
    pick = jnp.concatenate([onehot(lane.astype(f32) == span), onehot((lane + LANES).astype(f32) == span)], axis=1)
    chooser = onehot(((lane < 8) & (seq == (lane + 1).astype(f32))) | ((lane >= 8) & (lane < 16) & (rank == lane - 8)))
    found = dot(pick, by_span)
    mine = seq == lane_seq
    kept = [jnp.where(mine, found[:, i : i + LANES], 0.0).astype(bf16) for i in range(0, width, LANES)]
    packed = dot(jnp.concatenate(kept + [chooser], axis=1), fold)
    out_ref[...] = (packed + meta_scr[...]).astype(bf16)


def holder_kernel(
    pos_hbm, query_hbm, latent_hbm, key_up_hbm, chosen_hbm, slot_hbm, row_hbm, column_hbm, out_ref,
    pos_ref, query_ref, latent_ref, key_up_ref, chosen_ref, slot_ref, row_ref, column_ref, sems,
    angle_scr, q_scr, q_out, up_scr, cos_scr, sin_scr, slot_scr, span_scr, seq_scr, meta_scr, mask_scr, score_scr, turned_scr, turned_keys,
):
    small = [
        pltpu.make_async_copy(source, target, sems.at[i])
        for i, (source, target) in enumerate(
            [
                (chosen_hbm, chosen_ref),
                (slot_hbm, slot_ref),
                (pos_hbm, pos_ref),
                (row_hbm, row_ref),
                (column_hbm, column_ref),
                (query_hbm, query_ref),
                (key_up_hbm, key_up_ref),
            ]
        )
    ]
    for copy in small:
        copy.start()
    latents = [pltpu.make_async_copy(latent_hbm.at[s], latent_ref.at[s], sems.at[len(small) + s]) for s in range(SEQS)]
    for copy in latents:
        copy.start()
    for copy in small:
        copy.wait()
    pool = lax.axis_index("z") * 4 + lax.axis_index("xb") * 2 + lax.axis_index("side")
    plan(pool, chosen_ref, slot_ref, slot_scr, span_scr, seq_scr, meta_scr, mask_scr)
    rotate_queries(pos_ref, query_ref, row_ref, angle_scr, q_scr, q_out)
    key_angles(pool, column_ref, cos_scr, sin_scr)
    up_scr[...] = key_up_ref[...].astype(f32).T.astype(bf16)
    for copy in latents:
        copy.wait()
    levels = score_all(turned_keys, latent_ref, up_scr, q_out, cos_scr, sin_scr, mask_scr, score_scr)
    pack_rows(score_scr, turned_scr, levels, span_scr, seq_scr, meta_scr, out_ref)


def score_all(turned_keys, latent_ref, up_scr, q_out, cos_scr, sin_scr, mask_scr, score_scr):
    up = up_scr[...]
    cosine, sine = cos_scr[...], sin_scr[...]
    lane = iota((HEADS, LANES), 1)
    levels = jnp.zeros((HEADS, LANES), f32)
    for s in range(SEQS):
        for at in range(0, TOKENS, 256):
            keys = dot(up, latent_ref[s, :, at : at + 256])
            a, b = keys[:HALF], keys[HALF:]
            co, si = cos_scr[:, at : at + 256], sin_scr[:, at : at + 256]
            turned_keys[s * HD : s * HD + HALF, at : at + 256] = (a * co - b * si).astype(bf16)
            turned_keys[s * HD + HALF : (s + 1) * HD, at : at + 256] = (b * co + a * si).astype(bf16)
    gap = jnp.zeros((HEADS, HD), f32)
    spread = [jnp.concatenate([q_out[s] if i == s else gap for i in range(SEQS)], axis=1) for s in range(SEQS)]
    every = dot(jnp.concatenate(spread, axis=0).astype(bf16), turned_keys[...]) * (1.0 / math.sqrt(HD))
    for s in range(SEQS):
        scores = every[s * HEADS : (s + 1) * HEADS]
        live = jnp.concatenate([mask_scr[2 * s : 2 * s + 1, :], mask_scr[2 * s + 1 : 2 * s + 2, :]], axis=1) > 0.5
        peak = jnp.max(jnp.where(live, scores, BIG_NEG), axis=1, keepdims=True)
        weights = jnp.where(live, jnp.exp(scores - peak), 0.0)
        total = jnp.sum(weights, axis=1, keepdims=True)
        some = total > 0.0
        safe = jnp.where(some, total, 1.0)
        score_scr[s * HEADS : (s + 1) * HEADS, :] = weights * (1.0 / safe)
        levels = jnp.where(lane == s, jnp.where(some, peak + jnp.log(safe), BIG_NEG), levels)
    return levels


def owner_kernel(packed_ref, values_ref, out_ref, slot_vec, slot_sca, sem, found_scr, left_scr, sum_scr):
    rows = packed_ref[...]
    pick = iota((8, LANES), 1)
    slots = dot_nt(jnp.where(pick == 88, 64.0, jnp.where(pick == 89, 1.0, 0.0)).astype(bf16), rows)
    slot_vec[...] = slots[:1].astype(jnp.int32)
    copy = pltpu.make_async_copy(slot_vec, slot_sca, sem)
    copy.start()
    packed = dot_nt(onehot(iota((LANES, LANES), 0) == iota((LANES, LANES), 1)), rows)
    seq = packed[90:91]
    live = seq > 0.5
    mine = [seq == float(s + 1) for s in range(SEQS)]
    level = packed[64:72] + packed[72:80] + packed[80:88]
    every = packed[96:104] + packed[104:112] + packed[112:120]
    rank = iota((1, ROWS), 1) & (CAP - 1)
    level_of = jnp.zeros_like(level)
    for s in range(SEQS):
        here = rank == s
        top = jnp.max(jnp.where(here, every, BIG_NEG), axis=1, keepdims=True)
        total = jnp.sum(jnp.where(here, jnp.exp(every - top), 0.0), axis=1, keepdims=True)
        level_of = jnp.where(mine[s], top + jnp.log(total), level_of)
    factor = jnp.where(live, jnp.exp(level - level_of), 0.0)
    weights = [packed[t * HEADS : (t + 1) * HEADS] * factor for t in range(SPAN)]
    left = [jnp.concatenate([jnp.where(mine[s], weights[t], 0.0) for s in range(SEQS)], axis=0).astype(bf16) for t in range(SPAN)]
    left_scr[...] = jnp.concatenate(left, axis=1)
    copy.wait()

    @pl.loop(0, ROWS // BATCH)
    def _(step):
        for i in range(BATCH):
            row = step * BATCH + i
            found_scr[pl.ds(pl.multiple_of(row * SPAN, SPAN), SPAN), :] = values_ref[slot_sca[0, row]].astype(f32)

    right = [found_scr[pl.ds(t, ROWS, stride=SPAN), :].astype(bf16) for t in range(SPAN)]
    sum_scr[...] = dot(left_scr[...], jnp.concatenate(right, axis=0))
    result = jnp.concatenate([sum_scr[pl.ds(h, SEQS, stride=HEADS), :] for h in range(HEADS)], axis=1).astype(bf16)
    for p in range(PAIRS):
        out_ref[p] = result


def combine_kernel(gathered_ref, *refs):
    *weight_refs, out_ref = refs
    total = gathered_ref[0].astype(f32)
    for p in range(1, PAIRS):
        total = total + gathered_ref[p].astype(f32)
    total = total.astype(bf16)
    side = lax.axis_index("side")
    groups = out_ref.shape[0] // 2
    for k in range(2):
        projected = dot(total, weight_refs[k][...])
        width = projected.shape[1] // groups
        for g in range(groups):
            at = g * width
            half = projected[:, at // LANES * LANES : (at // LANES + 1) * LANES]
            out_ref[(side ^ k) * groups + g] = pltpu.roll(half, (LANES - at % LANES) % LANES, 1)


def finish_kernel(parts_ref, out_ref):
    total = parts_ref[0]
    for g in range(1, parts_ref.shape[0]):
        total = total + parts_ref[g]
    out_ref[...] = total[:, : out_ref.shape[1]].astype(bf16)


def score(*operands):
    buffers = [pltpu.SMEM(operands[0].shape, jnp.int32)]
    buffers += [pltpu.VMEM(x.shape, x.dtype) for x in operands[1:]]
    return pl.pallas_call(
        holder_kernel,
        in_specs=[pl.BlockSpec(memory_space=pltpu.HBM)] * len(operands),
        out_specs=pl.BlockSpec(memory_space=pltpu.VMEM),
        out_shape=jax.ShapeDtypeStruct((ROWS, LANES), bf16),
        scratch_shapes=[
            *buffers,
            pltpu.SemaphoreType.DMA((len(operands) - 1 + SEQS,)),
            pltpu.VMEM((3, SEQS, LANES), f32),
            pltpu.VMEM((SEQS * HEADS, HD), f32),
            pltpu.VMEM((SEQS, HEADS, HD), f32),
            pltpu.VMEM((HD, RANK), bf16),
            pltpu.VMEM((HALF, TOKENS), f32),
            pltpu.VMEM((HALF, TOKENS), f32),
            pltpu.VMEM((CHUNKS, LANES), jnp.int32),
            pltpu.VMEM((ROWS, LANES), f32),
            pltpu.VMEM((ROWS, LANES), f32),
            pltpu.VMEM((ROWS, LANES), f32),
            pltpu.VMEM((CHUNKS, LANES * SPAN), f32),
            pltpu.VMEM((SEQS * HEADS, TOKENS), f32),
            pltpu.VMEM((TOKENS, LANES), f32),
            pltpu.VMEM((SEQS * HD, TOKENS), bf16),
        ],
        compiler_params=pltpu.CompilerParams(vmem_limit_bytes=32 << 20),
        name="score",
    )(*[pltpu.with_memory_space_constraint(x, pltpu.HBM) for x in operands])


def weigh(packed, values):
    return pl.pallas_call(
        owner_kernel,
        in_specs=[pl.BlockSpec(memory_space=pltpu.VMEM)] * 2,
        out_specs=pl.BlockSpec(memory_space=pltpu.VMEM),
        out_shape=jax.ShapeDtypeStruct((PAIRS, SEQS, HEADS * HD), bf16),
        scratch_shapes=[
            pltpu.VMEM((1, ROWS), jnp.int32),
            pltpu.SMEM((1, ROWS), jnp.int32),
            pltpu.SemaphoreType.DMA,
            pltpu.VMEM((ROWS * SPAN, HD), f32),
            pltpu.VMEM((SEQS * HEADS, ROWS * SPAN), bf16),
            pltpu.VMEM((SEQS * HEADS, HD), f32),
        ],
        compiler_params=pltpu.CompilerParams(vmem_limit_bytes=24 << 20),
        name="weigh",
    )(packed, values)


def combine(gathered, weights, groups):
    return pl.pallas_call(
        combine_kernel,
        in_specs=[pl.BlockSpec(memory_space=pltpu.VMEM)] * 3,
        out_specs=pl.BlockSpec(memory_space=pltpu.VMEM),
        out_shape=jax.ShapeDtypeStruct((2 * groups, SEQS, LANES), f32),
        compiler_params=pltpu.CompilerParams(vmem_limit_bytes=16 << 20),
        name="combine",
    )(gathered, *weights)


def finish(parts, width):
    return pl.pallas_call(
        finish_kernel,
        in_specs=[pl.BlockSpec(memory_space=pltpu.VMEM)],
        out_specs=pl.BlockSpec(memory_space=pltpu.VMEM),
        out_shape=jax.ShapeDtypeStruct((SEQS, width), bf16),
        compiler_params=pltpu.CompilerParams(vmem_limit_bytes=8 << 20),
        name="finish",
    )(parts)


def on_device(query, query_pos, key_latent, key_up, value_cache, chosen, value_slot, out_weight):
    row_table, column_table = angle_tables()
    latent = jnp.swapaxes(key_latent, 1, 2)
    slot_rows = value_slot.reshape(-1, LANES)
    weights = [out_weight, lax.ppermute(out_weight, "side", [(0, 1), (1, 0)])]
    packed = score(query_pos, query, latent, key_up, chosen, slot_rows, row_table, column_table)
    arrived = lax.all_to_all(packed.reshape(POOLS, CAP, LANES), ("z", "xb", "side"), split_axis=0, concat_axis=0, tiled=True)
    arrived, weights[1] = lax.optimization_barrier((arrived, weights[1]))
    partial = weigh(arrived.reshape(ROWS, LANES), value_cache)
    gathered = lax.all_to_all(partial, ("xb", "z"), split_axis=0, concat_axis=0, tiled=True)
    groups = lax.axis_size("head")
    projected = combine(gathered, weights, groups)
    parts = lax.all_to_all(projected, ("side", "head"), split_axis=0, concat_axis=0, tiled=True)
    return finish(parts, out_weight.shape[1] // groups)


def solution(mesh):
    split = Mesh(mesh.devices.reshape(8, 2, 2, -1), ("z", "xb", "side", "head"))
    placed = (
        P(None, "head"),
        P(),
        P(None, ("z", "xb", "side"), None),
        P(None, "head"),
        P(("z", "xb", "side"), None, "head"),
        P(),
        P(),
        P("head", ("z", "xb", "side")),
    )
    return jax.shard_map(
        on_device, mesh=split, in_specs=placed, out_specs=P(None, ("z", "xb", "side", "head")), check_vma=False
    )
```

```python
import math

import jax
import jax.numpy as jnp
import numpy as np
from jax import lax
from jax.experimental import pallas as pl
from jax.experimental.pallas import tpu as pltpu
from jax.sharding import Mesh
from jax.sharding import PartitionSpec as P

SEQS = 8
HEADS = 8
HD = 128
HALF = HD // 2
RANK = 160
SPAN = 8
THETA = 500000.0
LANES = 128

POOLS = 32
PAIRS = POOLS // 2
CAP = 16
ROWS = POOLS * CAP
SPANS = 256
TOKENS = SPANS * SPAN
SLOTS = 2048
CHUNKS = SEQS * SPANS // LANES
BIG_NEG = -1e30
BATCH = 512

f32 = jnp.float32
bf16 = jnp.bfloat16

HI_ROWS, MID_ROWS, LO_ROWS = 40, 16, 128
MID_AT, LO_AT = HI_ROWS, HI_ROWS + MID_ROWS


def angle_tables():
    inverse = np.exp(-(2.0 * np.arange(HALF) / HD) * math.log(THETA))
    rows = np.concatenate([np.arange(HI_ROWS) * 2048.0, np.arange(MID_ROWS) * 128.0, np.arange(LO_ROWS) * 1.0])
    angles = rows[:, None] * inverse[None, :]
    row_table = np.concatenate([np.cos(angles), np.sin(angles)], axis=1).astype(np.float32)
    lanes = np.arange(LANES)
    columns = np.concatenate([np.minimum(lanes, HI_ROWS - 1) * 2048.0, np.minimum(lanes, MID_ROWS - 1) * 128.0, lanes * 1.0])
    angles = inverse[:, None] * columns[None, :]
    column_table = np.concatenate([np.cos(angles), np.sin(angles)], axis=0).astype(np.float32)
    return row_table, column_table


def iota(shape, dim):
    return lax.broadcasted_iota(jnp.int32, shape, dim)


def onehot(condition):
    return jnp.where(condition, 1.0, 0.0).astype(bf16)


def dot(a, b):
    return lax.dot_general(a, b, (((1,), (0,)), ((), ())), preferred_element_type=f32)


def dot_nt(a, b):
    return lax.dot_general(a, b, (((1,), (1,)), ((), ())), preferred_element_type=f32)


def pieces_of(x):
    first = x.astype(bf16).astype(f32)
    rest = x - first
    second = rest.astype(bf16).astype(f32)
    return first, second, rest - second


def rotate_queries(pos_ref, query_ref, row_ref, angle_scr, q_scr, q_out):
    for s in range(SEQS):
        pos = pos_ref[s]
        angle_scr[0, s : s + 1, :] = row_ref[pl.ds(pos >> 11, 1), :]
        angle_scr[1, s : s + 1, :] = row_ref[pl.ds(MID_AT + ((pos >> 7) & 15), 1), :]
        angle_scr[2, s : s + 1, :] = row_ref[pl.ds(LO_AT + (pos & 127), 1), :]
    first, second, third = angle_scr[0], angle_scr[1], angle_scr[2]
    cosine = first[:, :HALF] * second[:, :HALF] - first[:, HALF:] * second[:, HALF:]
    sine = first[:, HALF:] * second[:, :HALF] + first[:, :HALF] * second[:, HALF:]
    cosine, sine = (
        cosine * third[:, :HALF] - sine * third[:, HALF:],
        sine * third[:, :HALF] + cosine * third[:, HALF:],
    )
    for h in range(HEADS):
        rows = query_ref[:, h * HD : (h + 1) * HD].astype(f32)
        a, b = rows[:, :HALF], rows[:, HALF:]
        turned = jnp.concatenate([a * cosine - b * sine, b * cosine + a * sine], axis=1)
        q_scr[h * SEQS : (h + 1) * SEQS, :] = turned.astype(bf16).astype(f32)
    for s in range(SEQS):
        q_out[s] = q_scr[pl.ds(s, HEADS, stride=SEQS), :]


def key_angles(pool, column_ref, cos_scr, sin_scr):
    lane = iota((HD, LANES), 1)
    base = jnp.sum(jnp.where(lane == pool, column_ref[:, :LANES], 0.0), axis=1, keepdims=True)
    cp, sp = base[:HALF], base[HALF:]
    c2, s2 = column_ref[:HALF, LANES : 2 * LANES], column_ref[HALF:, LANES : 2 * LANES]
    cb, sb = cp * c2 - sp * s2, sp * c2 + cp * s2
    c3, s3 = column_ref[:HALF, 2 * LANES :], column_ref[HALF:, 2 * LANES :]
    for c in range(TOKENS // LANES):
        ca, sa = cb[:, c : c + 1], sb[:, c : c + 1]
        cos_scr[:, c * LANES : (c + 1) * LANES] = ca * c3 - sa * s3
        sin_scr[:, c * LANES : (c + 1) * LANES] = sa * c3 + ca * s3


def plan(rest, pool, chosen_ref, slot_ref, slot_scr, span_scr, seq_scr, meta_scr, mask_scr):
    relative = chosen_ref[...] - pool * SPANS
    here = (relative >= 0) & (relative < SPANS)
    row_code = jnp.where(here, 2 * iota(relative.shape, 0) + (relative >> 7), -1)
    lane_code = relative & 127
    picks = relative.shape[1]
    left = [onehot(iota((CHUNKS, picks), 0) == row_code[s : s + 1, :]) for s in range(SEQS)]
    right = [onehot(iota((LANES, picks), 0) == lane_code[s : s + 1, :]) for s in range(SEQS)]
    member = dot_nt(jnp.concatenate(left, axis=1), jnp.concatenate(right, axis=1))
    mask_scr[...] = dot(member.astype(bf16), onehot(iota((LANES, LANES * SPAN), 0) == (iota((LANES, LANES * SPAN), 1) >> 3)))
    for copy in rest:
        copy.wait()
    for s in range(SEQS):
        slot_scr[2 * s : 2 * s + 2, :] = slot_ref[pl.ds(s * (SPANS * POOLS // LANES) + 2 * pool, 2), :]
    slots = slot_scr[...]
    owner = jnp.where(member > 0.5, slots >> 11, -1)
    local_slot = slots & (SLOTS - 1)
    owners = [jnp.where(iota((POOLS, LANES), 0) == owner[c : c + 1, :], 1.0, 0.0) for c in range(CHUNKS)]
    earlier = iota((LANES, 2 * LANES), 0) < iota((LANES, 2 * LANES), 1)
    counted = dot(jnp.concatenate(owners, axis=0).astype(bf16), onehot(earlier))
    carry = jnp.zeros((POOLS, LANES), f32)
    facts = []
    for c in range(CHUNKS):
        part = counted[c * POOLS : (c + 1) * POOLS]
        rank = jnp.sum(owners[c] * (part[:, :LANES] + carry), axis=0, keepdims=True).astype(jnp.int32)
        carry = carry + part[:, LANES:]
        at_rank = jnp.where(iota((CAP, LANES), 0) == rank, 1.0, 0.0)
        span = (iota((1, LANES), 1) + (c % 2) * LANES).astype(f32)
        slot = local_slot[c : c + 1, :]
        facts.append(
            jnp.concatenate(
                [
                    at_rank * span,
                    at_rank * float(c // 2 + 1),
                    at_rank * (slot >> 6).astype(f32),
                    at_rank * (slot & 63).astype(f32),
                ],
                axis=0,
            )
        )
    table = dot_nt(
        jnp.concatenate(owners, axis=1).astype(bf16), jnp.concatenate(facts, axis=1).astype(bf16)
    )
    spread = dot(onehot((iota((ROWS, POOLS), 0) >> 4) == iota((ROWS, POOLS), 1)), table.astype(bf16))
    own = (iota(spread.shape, 1) & (CAP - 1)) == (iota(spread.shape, 0) & (CAP - 1))
    kind = iota((4 * CAP, 3 * LANES), 0) >> 4
    column = iota((4 * CAP, 3 * LANES), 1)
    fold = onehot(
        ((column < LANES) & (kind == 0))
        | ((column >= LANES) & (column < 2 * LANES) & (kind == 1))
        | ((column == 2 * LANES + 88) & (kind == 2))
        | ((column == 2 * LANES + 89) & (kind == 3))
        | ((column == 2 * LANES + 90) & (kind == 1))
    )
    known = dot(jnp.where(own, spread, 0.0).astype(bf16), fold)
    span_scr[...] = known[:, :LANES]
    seq_scr[...] = known[:, LANES : 2 * LANES]
    meta_scr[...] = known[:, 2 * LANES :]


def pack_rows(score_scr, turned_scr, levels, span_scr, seq_scr, meta_scr, out_ref):
    weights = score_scr[...]
    turned_scr[...] = jnp.concatenate([weights, weights], axis=0).T
    low = iota((SPANS, LANES), 1) < 64
    parts = [
        jnp.where(low, turned_scr[pl.ds(t, SPANS, stride=SPAN), :], turned_scr[pl.ds(t + 1, SPANS, stride=SPAN), :])
        for t in range(0, SPAN, 2)
    ]
    by_span = jnp.concatenate(parts, axis=1).astype(bf16)
    width = by_span.shape[1]
    source = iota((width, LANES), 0)
    target = iota((width, LANES), 1)
    fold = onehot((target < 64) & ((source >> 6) == (target >> 3)) & ((source & 7) == (target & 7)))
    first, second, third = pieces_of(levels)
    own = jnp.concatenate([first, second, third], axis=0)
    gap = jnp.zeros((8, LANES), f32)
    table = jnp.concatenate([gap] * 8 + [own, gap, pltpu.roll(own, 8, 1), gap], axis=0)
    fold = jnp.concatenate([fold, table.T.astype(bf16)], axis=0)
    lane = iota((ROWS, LANES), 1)
    lane_seq = ((lane & 63) >> 3).astype(f32) + 1.0
    rank = iota((ROWS, LANES), 0) & (CAP - 1)
    span = span_scr[...]
    seq = seq_scr[...]
    pick = jnp.concatenate([onehot(lane.astype(f32) == span), onehot((lane + LANES).astype(f32) == span)], axis=1)
    chooser = onehot(((lane < 8) & (seq == (lane + 1).astype(f32))) | ((lane >= 8) & (lane < 16) & (rank == lane - 8)))
    found = dot(pick, by_span)
    mine = seq == lane_seq
    kept = [jnp.where(mine, found[:, i : i + LANES], 0.0).astype(bf16) for i in range(0, width, LANES)]
    packed = dot(jnp.concatenate(kept + [chooser], axis=1), fold)
    out_ref[...] = (packed + meta_scr[...]).astype(bf16)


def holder_kernel(
    pos_hbm, query_hbm, latent_hbm, key_up_hbm, chosen_hbm, slot_hbm, row_hbm, column_hbm, out_ref,
    pos_ref, query_ref, latent_ref, key_up_ref, chosen_ref, slot_ref, row_ref, column_ref, sems,
    angle_scr, q_scr, q_out, up_scr, cos_scr, sin_scr, slot_scr, span_scr, seq_scr, meta_scr, mask_scr, score_scr, turned_scr, turned_keys,
):
    small = [
        pltpu.make_async_copy(source, target, sems.at[i])
        for i, (source, target) in enumerate(
            [
                (chosen_hbm, chosen_ref),
                (slot_hbm, slot_ref),
                (pos_hbm, pos_ref),
                (row_hbm, row_ref),
                (column_hbm, column_ref),
                (query_hbm, query_ref),
                (key_up_hbm, key_up_ref),
            ]
        )
    ]
    for copy in small:
        copy.start()
    latents = [pltpu.make_async_copy(latent_hbm.at[s], latent_ref.at[s], sems.at[len(small) + s]) for s in range(SEQS)]
    for copy in latents:
        copy.start()
    small[0].wait()
    pool = lax.axis_index("z") * 4 + lax.axis_index("xb") * 2 + lax.axis_index("side")
    plan(small[1:], pool, chosen_ref, slot_ref, slot_scr, span_scr, seq_scr, meta_scr, mask_scr)
    rotate_queries(pos_ref, query_ref, row_ref, angle_scr, q_scr, q_out)
    key_angles(pool, column_ref, cos_scr, sin_scr)
    up_scr[...] = key_up_ref[...].astype(f32).T.astype(bf16)
    for copy in latents:
        copy.wait()
    levels = score_all(turned_keys, latent_ref, up_scr, q_out, cos_scr, sin_scr, mask_scr, score_scr)
    pack_rows(score_scr, turned_scr, levels, span_scr, seq_scr, meta_scr, out_ref)


def score_all(turned_keys, latent_ref, up_scr, q_out, cos_scr, sin_scr, mask_scr, score_scr):
    up = up_scr[...]
    cosine, sine = cos_scr[...], sin_scr[...]
    lane = iota((HEADS, LANES), 1)
    levels = jnp.zeros((HEADS, LANES), f32)
    for s in range(SEQS):
        for at in range(0, TOKENS, 256):
            keys = dot(up, latent_ref[s, :, at : at + 256])
            a, b = keys[:HALF], keys[HALF:]
            co, si = cos_scr[:, at : at + 256], sin_scr[:, at : at + 256]
            turned_keys[s * HD : s * HD + HALF, at : at + 256] = (a * co - b * si).astype(bf16)
            turned_keys[s * HD + HALF : (s + 1) * HD, at : at + 256] = (b * co + a * si).astype(bf16)
    gap = jnp.zeros((HEADS, HD), f32)
    spread = [jnp.concatenate([q_out[s] if i == s else gap for i in range(SEQS)], axis=1) for s in range(SEQS)]
    every = dot(jnp.concatenate(spread, axis=0).astype(bf16), turned_keys[...]) * (1.0 / math.sqrt(HD))
    for s in range(SEQS):
        scores = every[s * HEADS : (s + 1) * HEADS]
        live = jnp.concatenate([mask_scr[2 * s : 2 * s + 1, :], mask_scr[2 * s + 1 : 2 * s + 2, :]], axis=1) > 0.5
        peak = jnp.max(jnp.where(live, scores, BIG_NEG), axis=1, keepdims=True)
        weights = jnp.where(live, jnp.exp(scores - peak), 0.0)
        total = jnp.sum(weights, axis=1, keepdims=True)
        some = total > 0.0
        safe = jnp.where(some, total, 1.0)
        score_scr[s * HEADS : (s + 1) * HEADS, :] = weights * (1.0 / safe)
        levels = jnp.where(lane == s, jnp.where(some, peak + jnp.log(safe), BIG_NEG), levels)
    return levels


def owner_kernel(packed_ref, values_ref, out_ref, slot_vec, slot_sca, sem, found_scr, left_scr, sum_scr):
    rows = packed_ref[...]
    pick = iota((8, LANES), 1)
    slots = dot_nt(jnp.where(pick == 88, 64.0, jnp.where(pick == 89, 1.0, 0.0)).astype(bf16), rows)
    slot_vec[...] = slots[:1].astype(jnp.int32)
    copy = pltpu.make_async_copy(slot_vec, slot_sca, sem)
    copy.start()
    packed = dot_nt(onehot(iota((LANES, LANES), 0) == iota((LANES, LANES), 1)), rows)
    seq = packed[90:91]
    live = seq > 0.5
    mine = [seq == float(s + 1) for s in range(SEQS)]
    level = packed[64:72] + packed[72:80] + packed[80:88]
    every = packed[96:104] + packed[104:112] + packed[112:120]
    rank = iota((1, ROWS), 1) & (CAP - 1)
    level_of = jnp.zeros_like(level)
    for s in range(SEQS):
        here = rank == s
        top = jnp.max(jnp.where(here, every, BIG_NEG), axis=1, keepdims=True)
        total = jnp.sum(jnp.where(here, jnp.exp(every - top), 0.0), axis=1, keepdims=True)
        level_of = jnp.where(mine[s], top + jnp.log(total), level_of)
    factor = jnp.where(live, jnp.exp(level - level_of), 0.0)
    weights = [packed[t * HEADS : (t + 1) * HEADS] * factor for t in range(SPAN)]
    left = [jnp.concatenate([jnp.where(mine[s], weights[t], 0.0) for s in range(SEQS)], axis=0).astype(bf16) for t in range(SPAN)]
    left_scr[...] = jnp.concatenate(left, axis=1)
    copy.wait()

    @pl.loop(0, ROWS // BATCH)
    def _(step):
        for i in range(BATCH):
            row = step * BATCH + i
            found_scr[pl.ds(pl.multiple_of(row * SPAN, SPAN), SPAN), :] = values_ref[slot_sca[0, row]].astype(f32)

    right = [found_scr[pl.ds(t, ROWS, stride=SPAN), :].astype(bf16) for t in range(SPAN)]
    sum_scr[...] = dot(left_scr[...], jnp.concatenate(right, axis=0))
    result = jnp.concatenate([sum_scr[pl.ds(h, SEQS, stride=HEADS), :] for h in range(HEADS)], axis=1).astype(bf16)
    for p in range(PAIRS):
        out_ref[p] = result


def combine_kernel(gathered_ref, *refs):
    *weight_refs, out_ref = refs
    total = gathered_ref[0].astype(f32)
    for p in range(1, PAIRS):
        total = total + gathered_ref[p].astype(f32)
    total = total.astype(bf16)
    side = lax.axis_index("side")
    groups = out_ref.shape[0] // 2
    for k in range(2):
        projected = dot(total, weight_refs[k][...])
        width = projected.shape[1] // groups
        for g in range(groups):
            at = g * width
            half = projected[:, at // LANES * LANES : (at // LANES + 1) * LANES]
            out_ref[(side ^ k) * groups + g] = pltpu.roll(half, (LANES - at % LANES) % LANES, 1)


def finish_kernel(parts_ref, out_ref):
    total = parts_ref[0]
    for g in range(1, parts_ref.shape[0]):
        total = total + parts_ref[g]
    out_ref[...] = total[:, : out_ref.shape[1]].astype(bf16)


def score(*operands):
    buffers = [pltpu.SMEM(operands[0].shape, jnp.int32)]
    buffers += [pltpu.VMEM(x.shape, x.dtype) for x in operands[1:]]
    return pl.pallas_call(
        holder_kernel,
        in_specs=[pl.BlockSpec(memory_space=pltpu.HBM)] * len(operands),
        out_specs=pl.BlockSpec(memory_space=pltpu.VMEM),
        out_shape=jax.ShapeDtypeStruct((ROWS, LANES), bf16),
        scratch_shapes=[
            *buffers,
            pltpu.SemaphoreType.DMA((len(operands) - 1 + SEQS,)),
            pltpu.VMEM((3, SEQS, LANES), f32),
            pltpu.VMEM((SEQS * HEADS, HD), f32),
            pltpu.VMEM((SEQS, HEADS, HD), f32),
            pltpu.VMEM((HD, RANK), bf16),
            pltpu.VMEM((HALF, TOKENS), f32),
            pltpu.VMEM((HALF, TOKENS), f32),
            pltpu.VMEM((CHUNKS, LANES), jnp.int32),
            pltpu.VMEM((ROWS, LANES), f32),
            pltpu.VMEM((ROWS, LANES), f32),
            pltpu.VMEM((ROWS, LANES), f32),
            pltpu.VMEM((CHUNKS, LANES * SPAN), f32),
            pltpu.VMEM((SEQS * HEADS, TOKENS), f32),
            pltpu.VMEM((TOKENS, LANES), f32),
            pltpu.VMEM((SEQS * HD, TOKENS), bf16),
        ],
        compiler_params=pltpu.CompilerParams(vmem_limit_bytes=32 << 20),
        name="score",
    )(*[pltpu.with_memory_space_constraint(x, pltpu.HBM) for x in operands])


def weigh(packed, values):
    return pl.pallas_call(
        owner_kernel,
        in_specs=[pl.BlockSpec(memory_space=pltpu.VMEM)] * 2,
        out_specs=pl.BlockSpec(memory_space=pltpu.VMEM),
        out_shape=jax.ShapeDtypeStruct((PAIRS, SEQS, HEADS * HD), bf16),
        scratch_shapes=[
            pltpu.VMEM((1, ROWS), jnp.int32),
            pltpu.SMEM((1, ROWS), jnp.int32),
            pltpu.SemaphoreType.DMA,
            pltpu.VMEM((ROWS * SPAN, HD), f32),
            pltpu.VMEM((SEQS * HEADS, ROWS * SPAN), bf16),
            pltpu.VMEM((SEQS * HEADS, HD), f32),
        ],
        compiler_params=pltpu.CompilerParams(vmem_limit_bytes=24 << 20),
        name="weigh",
    )(packed, values)


def combine(gathered, weights, groups):
    return pl.pallas_call(
        combine_kernel,
        in_specs=[pl.BlockSpec(memory_space=pltpu.VMEM)] * 3,
        out_specs=pl.BlockSpec(memory_space=pltpu.VMEM),
        out_shape=jax.ShapeDtypeStruct((2 * groups, SEQS, LANES), f32),
        compiler_params=pltpu.CompilerParams(vmem_limit_bytes=16 << 20),
        name="combine",
    )(gathered, *weights)


def finish(parts, width):
    return pl.pallas_call(
        finish_kernel,
        in_specs=[pl.BlockSpec(memory_space=pltpu.VMEM)],
        out_specs=pl.BlockSpec(memory_space=pltpu.VMEM),
        out_shape=jax.ShapeDtypeStruct((SEQS, width), bf16),
        compiler_params=pltpu.CompilerParams(vmem_limit_bytes=8 << 20),
        name="finish",
    )(parts)


def on_device(query, query_pos, key_latent, key_up, value_cache, chosen, value_slot, out_weight):
    row_table, column_table = angle_tables()
    latent = jnp.swapaxes(key_latent, 1, 2)
    slot_rows = value_slot.reshape(-1, LANES)
    weights = [out_weight, lax.ppermute(out_weight, "side", [(0, 1), (1, 0)])]
    packed = score(query_pos, query, latent, key_up, chosen, slot_rows, row_table, column_table)
    arrived = lax.all_to_all(packed.reshape(POOLS, CAP, LANES), ("z", "xb", "side"), split_axis=0, concat_axis=0, tiled=True)
    arrived, weights[1] = lax.optimization_barrier((arrived, weights[1]))
    partial = weigh(arrived.reshape(ROWS, LANES), value_cache)
    gathered = lax.all_to_all(partial, ("xb", "z"), split_axis=0, concat_axis=0, tiled=True)
    groups = lax.axis_size("head")
    projected = combine(gathered, weights, groups)
    parts = lax.all_to_all(projected, ("side", "head"), split_axis=0, concat_axis=0, tiled=True)
    return finish(parts, out_weight.shape[1] // groups)


def solution(mesh):
    split = Mesh(mesh.devices.reshape(8, 2, 2, -1), ("z", "xb", "side", "head"))
    placed = (
        P(None, "head"),
        P(),
        P(None, ("z", "xb", "side"), None),
        P(None, "head"),
        P(("z", "xb", "side"), None, "head"),
        P(),
        P(),
        P("head", ("z", "xb", "side")),
    )
    return jax.shard_map(
        on_device, mesh=split, in_specs=placed, out_specs=P(None, ("z", "xb", "side", "head")), check_vma=False
    )
```

```python
import math

import jax
import jax.numpy as jnp
import numpy as np
from jax import lax
from jax.experimental import pallas as pl
from jax.experimental.pallas import tpu as pltpu
from jax.sharding import Mesh
from jax.sharding import PartitionSpec as P

SEQS = 8
HEADS = 8
HD = 128
HALF = HD // 2
RANK = 160
SPAN = 8
THETA = 500000.0
LANES = 128

POOLS = 32
PAIRS = POOLS // 2
CAP = 16
ROWS = POOLS * CAP
SPANS = 256
TOKENS = SPANS * SPAN
SLOTS = 2048
CHUNKS = SEQS * SPANS // LANES
BIG_NEG = -1e30
BATCH = 512

f32 = jnp.float32
bf16 = jnp.bfloat16

HI_ROWS, MID_ROWS, LO_ROWS = 40, 16, 128
MID_AT, LO_AT = HI_ROWS, HI_ROWS + MID_ROWS


def angle_tables():
    inverse = np.exp(-(2.0 * np.arange(HALF) / HD) * math.log(THETA))
    rows = np.concatenate([np.arange(HI_ROWS) * 2048.0, np.arange(MID_ROWS) * 128.0, np.arange(LO_ROWS) * 1.0])
    angles = rows[:, None] * inverse[None, :]
    row_table = np.concatenate([np.cos(angles), np.sin(angles)], axis=1).astype(np.float32)
    lanes = np.arange(LANES)
    columns = np.concatenate([np.minimum(lanes, HI_ROWS - 1) * 2048.0, np.minimum(lanes, MID_ROWS - 1) * 128.0, lanes * 1.0])
    angles = inverse[:, None] * columns[None, :]
    column_table = np.concatenate([np.cos(angles), np.sin(angles)], axis=0).astype(np.float32)
    return row_table, column_table


def iota(shape, dim):
    return lax.broadcasted_iota(jnp.int32, shape, dim)


def onehot(condition):
    return jnp.where(condition, 1.0, 0.0).astype(bf16)


def dot(a, b):
    return lax.dot_general(a, b, (((1,), (0,)), ((), ())), preferred_element_type=f32)


def dot_nt(a, b):
    return lax.dot_general(a, b, (((1,), (1,)), ((), ())), preferred_element_type=f32)


def pieces_of(x):
    first = x.astype(bf16).astype(f32)
    rest = x - first
    second = rest.astype(bf16).astype(f32)
    return first, second, rest - second


def rotate_queries(pos_ref, query_ref, row_ref, angle_scr, q_scr, q_out):
    for s in range(SEQS):
        pos = pos_ref[s]
        angle_scr[0, s : s + 1, :] = row_ref[pl.ds(pos >> 11, 1), :]
        angle_scr[1, s : s + 1, :] = row_ref[pl.ds(MID_AT + ((pos >> 7) & 15), 1), :]
        angle_scr[2, s : s + 1, :] = row_ref[pl.ds(LO_AT + (pos & 127), 1), :]
    first, second, third = angle_scr[0], angle_scr[1], angle_scr[2]
    cosine = first[:, :HALF] * second[:, :HALF] - first[:, HALF:] * second[:, HALF:]
    sine = first[:, HALF:] * second[:, :HALF] + first[:, :HALF] * second[:, HALF:]
    cosine, sine = (
        cosine * third[:, :HALF] - sine * third[:, HALF:],
        sine * third[:, :HALF] + cosine * third[:, HALF:],
    )
    for h in range(HEADS):
        rows = query_ref[:, h * HD : (h + 1) * HD].astype(f32)
        a, b = rows[:, :HALF], rows[:, HALF:]
        turned = jnp.concatenate([a * cosine - b * sine, b * cosine + a * sine], axis=1)
        q_scr[h * SEQS : (h + 1) * SEQS, :] = turned.astype(bf16).astype(f32)
    for s in range(SEQS):
        q_out[s] = q_scr[pl.ds(s, HEADS, stride=SEQS), :]


def key_angles(pool, column_ref, cos_scr, sin_scr):
    lane = iota((HD, LANES), 1)
    base = jnp.sum(jnp.where(lane == pool, column_ref[:, :LANES], 0.0), axis=1, keepdims=True)
    cp, sp = base[:HALF], base[HALF:]
    c2, s2 = column_ref[:HALF, LANES : 2 * LANES], column_ref[HALF:, LANES : 2 * LANES]
    cb, sb = cp * c2 - sp * s2, sp * c2 + cp * s2
    c3, s3 = column_ref[:HALF, 2 * LANES :], column_ref[HALF:, 2 * LANES :]
    for c in range(TOKENS // LANES):
        ca, sa = cb[:, c : c + 1], sb[:, c : c + 1]
        cos_scr[:, c * LANES : (c + 1) * LANES] = ca * c3 - sa * s3
        sin_scr[:, c * LANES : (c + 1) * LANES] = sa * c3 + ca * s3


def plan(rest, pool, chosen_ref, slot_ref, slot_scr, span_scr, seq_scr, meta_scr, mask_scr):
    relative = chosen_ref[...] - pool * SPANS
    here = (relative >= 0) & (relative < SPANS)
    row_code = jnp.where(here, 2 * iota(relative.shape, 0) + (relative >> 7), -1)
    lane_code = relative & 127
    picks = relative.shape[1]
    left = [onehot(iota((CHUNKS, picks), 0) == row_code[s : s + 1, :]) for s in range(SEQS)]
    right = [onehot(iota((LANES, picks), 0) == lane_code[s : s + 1, :]) for s in range(SEQS)]
    member = dot_nt(jnp.concatenate(left, axis=1), jnp.concatenate(right, axis=1))
    mask_scr[...] = dot(member.astype(bf16), onehot(iota((LANES, LANES * SPAN), 0) == (iota((LANES, LANES * SPAN), 1) >> 3)))
    for copy in rest:
        copy.wait()
    for s in range(SEQS):
        slot_scr[2 * s : 2 * s + 2, :] = slot_ref[pl.ds(s * (SPANS * POOLS // LANES) + 2 * pool, 2), :]
    slots = slot_scr[...]
    owner = slots >> 11
    owner = jnp.where(member > 0.5, (owner & 3) * 8 + (owner >> 2), -1)
    local_slot = slots & (SLOTS - 1)
    owners = [jnp.where(iota((POOLS, LANES), 0) == owner[c : c + 1, :], 1.0, 0.0) for c in range(CHUNKS)]
    earlier = iota((LANES, 2 * LANES), 0) < iota((LANES, 2 * LANES), 1)
    counted = dot(jnp.concatenate(owners, axis=0).astype(bf16), onehot(earlier))
    carry = jnp.zeros((POOLS, LANES), f32)
    facts = []
    for c in range(CHUNKS):
        part = counted[c * POOLS : (c + 1) * POOLS]
        rank = jnp.sum(owners[c] * (part[:, :LANES] + carry), axis=0, keepdims=True).astype(jnp.int32)
        carry = carry + part[:, LANES:]
        at_rank = jnp.where(iota((CAP, LANES), 0) == rank, 1.0, 0.0)
        span = (iota((1, LANES), 1) + (c % 2) * LANES).astype(f32)
        slot = local_slot[c : c + 1, :]
        facts.append(
            jnp.concatenate(
                [
                    at_rank * span,
                    at_rank * float(c // 2 + 1),
                    at_rank * (slot >> 6).astype(f32),
                    at_rank * (slot & 63).astype(f32),
                ],
                axis=0,
            )
        )
    table = dot_nt(
        jnp.concatenate(owners, axis=1).astype(bf16), jnp.concatenate(facts, axis=1).astype(bf16)
    )
    spread = dot(onehot((iota((ROWS, POOLS), 0) >> 4) == iota((ROWS, POOLS), 1)), table.astype(bf16))
    own = (iota(spread.shape, 1) & (CAP - 1)) == (iota(spread.shape, 0) & (CAP - 1))
    kind = iota((4 * CAP, 3 * LANES), 0) >> 4
    column = iota((4 * CAP, 3 * LANES), 1)
    fold = onehot(
        ((column < LANES) & (kind == 0))
        | ((column >= LANES) & (column < 2 * LANES) & (kind == 1))
        | ((column == 2 * LANES + 88) & (kind == 2))
        | ((column == 2 * LANES + 89) & (kind == 3))
        | ((column == 2 * LANES + 90) & (kind == 1))
    )
    known = dot(jnp.where(own, spread, 0.0).astype(bf16), fold)
    span_scr[...] = known[:, :LANES]
    seq_scr[...] = known[:, LANES : 2 * LANES]
    meta_scr[...] = known[:, 2 * LANES :]


def pack_rows(score_scr, turned_scr, levels, span_scr, seq_scr, meta_scr, out_ref):
    weights = score_scr[...]
    turned_scr[...] = jnp.concatenate([weights, weights], axis=0).T
    low = iota((SPANS, LANES), 1) < 64
    parts = [
        jnp.where(low, turned_scr[pl.ds(t, SPANS, stride=SPAN), :], turned_scr[pl.ds(t + 1, SPANS, stride=SPAN), :])
        for t in range(0, SPAN, 2)
    ]
    by_span = jnp.concatenate(parts, axis=1).astype(bf16)
    width = by_span.shape[1]
    source = iota((width, LANES), 0)
    target = iota((width, LANES), 1)
    fold = onehot((target < 64) & ((source >> 6) == (target >> 3)) & ((source & 7) == (target & 7)))
    first, second, third = pieces_of(levels)
    own = jnp.concatenate([first, second, third], axis=0)
    gap = jnp.zeros((8, LANES), f32)
    table = jnp.concatenate([gap] * 8 + [own, gap, pltpu.roll(own, 8, 1), gap], axis=0)
    fold = jnp.concatenate([fold, table.T.astype(bf16)], axis=0)
    lane = iota((ROWS, LANES), 1)
    lane_seq = ((lane & 63) >> 3).astype(f32) + 1.0
    rank = iota((ROWS, LANES), 0) & (CAP - 1)
    span = span_scr[...]
    seq = seq_scr[...]
    pick = jnp.concatenate([onehot(lane.astype(f32) == span), onehot((lane + LANES).astype(f32) == span)], axis=1)
    chooser = onehot(((lane < 8) & (seq == (lane + 1).astype(f32))) | ((lane >= 8) & (lane < 16) & (rank == lane - 8)))
    found = dot(pick, by_span)
    mine = seq == lane_seq
    kept = [jnp.where(mine, found[:, i : i + LANES], 0.0).astype(bf16) for i in range(0, width, LANES)]
    packed = dot(jnp.concatenate(kept + [chooser], axis=1), fold)
    out_ref[...] = (packed + meta_scr[...]).astype(bf16)


def holder_kernel(
    pos_hbm, query_hbm, latent_hbm, key_up_hbm, chosen_hbm, slot_hbm, row_hbm, column_hbm, out_ref,
    pos_ref, query_ref, latent_ref, key_up_ref, chosen_ref, slot_ref, row_ref, column_ref, sems,
    angle_scr, q_scr, q_out, up_scr, cos_scr, sin_scr, slot_scr, span_scr, seq_scr, meta_scr, mask_scr, score_scr, turned_scr, turned_keys,
):
    small = [
        pltpu.make_async_copy(source, target, sems.at[i])
        for i, (source, target) in enumerate(
            [
                (chosen_hbm, chosen_ref),
                (slot_hbm, slot_ref),
                (pos_hbm, pos_ref),
                (row_hbm, row_ref),
                (column_hbm, column_ref),
                (query_hbm, query_ref),
                (key_up_hbm, key_up_ref),
            ]
        )
    ]
    for copy in small:
        copy.start()
    latents = [pltpu.make_async_copy(latent_hbm.at[s], latent_ref.at[s], sems.at[len(small) + s]) for s in range(SEQS)]
    for copy in latents:
        copy.start()
    small[0].wait()
    pool = lax.axis_index("z") * 4 + lax.axis_index("xb") * 2 + lax.axis_index("side")
    plan(small[1:], pool, chosen_ref, slot_ref, slot_scr, span_scr, seq_scr, meta_scr, mask_scr)
    rotate_queries(pos_ref, query_ref, row_ref, angle_scr, q_scr, q_out)
    key_angles(pool, column_ref, cos_scr, sin_scr)
    up_scr[...] = key_up_ref[...].astype(f32).T.astype(bf16)
    for copy in latents:
        copy.wait()
    levels = score_all(turned_keys, latent_ref, up_scr, q_out, cos_scr, sin_scr, mask_scr, score_scr)
    pack_rows(score_scr, turned_scr, levels, span_scr, seq_scr, meta_scr, out_ref)


def score_all(turned_keys, latent_ref, up_scr, q_out, cos_scr, sin_scr, mask_scr, score_scr):
    up = up_scr[...]
    cosine, sine = cos_scr[...], sin_scr[...]
    lane = iota((HEADS, LANES), 1)
    levels = jnp.zeros((HEADS, LANES), f32)
    for s in range(SEQS):
        for at in range(0, TOKENS, 256):
            keys = dot(up, latent_ref[s, :, at : at + 256])
            a, b = keys[:HALF], keys[HALF:]
            co, si = cos_scr[:, at : at + 256], sin_scr[:, at : at + 256]
            turned_keys[s * HD : s * HD + HALF, at : at + 256] = (a * co - b * si).astype(bf16)
            turned_keys[s * HD + HALF : (s + 1) * HD, at : at + 256] = (b * co + a * si).astype(bf16)
    gap = jnp.zeros((HEADS, HD), f32)
    spread = [jnp.concatenate([q_out[s] if i == s else gap for i in range(SEQS)], axis=1) for s in range(SEQS)]
    every = dot(jnp.concatenate(spread, axis=0).astype(bf16), turned_keys[...]) * (1.0 / math.sqrt(HD))
    for s in range(SEQS):
        scores = every[s * HEADS : (s + 1) * HEADS]
        live = jnp.concatenate([mask_scr[2 * s : 2 * s + 1, :], mask_scr[2 * s + 1 : 2 * s + 2, :]], axis=1) > 0.5
        peak = jnp.max(jnp.where(live, scores, BIG_NEG), axis=1, keepdims=True)
        weights = jnp.where(live, jnp.exp(scores - peak), 0.0)
        total = jnp.sum(weights, axis=1, keepdims=True)
        some = total > 0.0
        safe = jnp.where(some, total, 1.0)
        score_scr[s * HEADS : (s + 1) * HEADS, :] = weights * (1.0 / safe)
        levels = jnp.where(lane == s, jnp.where(some, peak + jnp.log(safe), BIG_NEG), levels)
    return levels


def owner_kernel(packed_ref, values_ref, out_ref, slot_vec, slot_sca, sem, found_scr, left_scr, sum_scr):
    rows = packed_ref[...]
    pick = iota((8, LANES), 1)
    slots = dot_nt(jnp.where(pick == 88, 64.0, jnp.where(pick == 89, 1.0, 0.0)).astype(bf16), rows)
    slot_vec[...] = slots[:1].astype(jnp.int32)
    copy = pltpu.make_async_copy(slot_vec, slot_sca, sem)
    copy.start()
    packed = dot_nt(onehot(iota((LANES, LANES), 0) == iota((LANES, LANES), 1)), rows)
    seq = packed[90:91]
    live = seq > 0.5
    mine = [seq == float(s + 1) for s in range(SEQS)]
    level = packed[64:72] + packed[72:80] + packed[80:88]
    every = packed[96:104] + packed[104:112] + packed[112:120]
    rank = iota((1, ROWS), 1) & (CAP - 1)
    level_of = jnp.zeros_like(level)
    for s in range(SEQS):
        here = rank == s
        top = jnp.max(jnp.where(here, every, BIG_NEG), axis=1, keepdims=True)
        total = jnp.sum(jnp.where(here, jnp.exp(every - top), 0.0), axis=1, keepdims=True)
        level_of = jnp.where(mine[s], top + jnp.log(total), level_of)
    factor = jnp.where(live, jnp.exp(level - level_of), 0.0)
    weights = [packed[t * HEADS : (t + 1) * HEADS] * factor for t in range(SPAN)]
    left = [jnp.concatenate([jnp.where(mine[s], weights[t], 0.0) for s in range(SEQS)], axis=0).astype(bf16) for t in range(SPAN)]
    left_scr[...] = jnp.concatenate(left, axis=1)
    copy.wait()

    @pl.loop(0, ROWS // BATCH)
    def _(step):
        for i in range(BATCH):
            row = step * BATCH + i
            found_scr[pl.ds(pl.multiple_of(row * SPAN, SPAN), SPAN), :] = values_ref[slot_sca[0, row]].astype(f32)

    right = [found_scr[pl.ds(t, ROWS, stride=SPAN), :].astype(bf16) for t in range(SPAN)]
    sum_scr[...] = dot(left_scr[...], jnp.concatenate(right, axis=0))
    result = jnp.concatenate([sum_scr[pl.ds(h, SEQS, stride=HEADS), :] for h in range(HEADS)], axis=1).astype(bf16)
    for p in range(PAIRS):
        out_ref[p] = result


def combine_kernel(gathered_ref, *refs):
    *weight_refs, out_ref = refs
    total = gathered_ref[0].astype(f32)
    for p in range(1, PAIRS):
        total = total + gathered_ref[p].astype(f32)
    total = total.astype(bf16)
    side = lax.axis_index("side")
    groups = out_ref.shape[0] // 2
    for k in range(2):
        projected = dot(total, weight_refs[k][...])
        width = projected.shape[1] // groups
        for g in range(groups):
            at = g * width
            half = projected[:, at // LANES * LANES : (at // LANES + 1) * LANES]
            out_ref[(side ^ k) * groups + g] = pltpu.roll(half, (LANES - at % LANES) % LANES, 1)


def finish_kernel(parts_ref, out_ref):
    total = parts_ref[0]
    for g in range(1, parts_ref.shape[0]):
        total = total + parts_ref[g]
    out_ref[...] = total[:, : out_ref.shape[1]].astype(bf16)


def score(*operands):
    buffers = [pltpu.SMEM(operands[0].shape, jnp.int32)]
    buffers += [pltpu.VMEM(x.shape, x.dtype) for x in operands[1:]]
    return pl.pallas_call(
        holder_kernel,
        in_specs=[pl.BlockSpec(memory_space=pltpu.HBM)] * len(operands),
        out_specs=pl.BlockSpec(memory_space=pltpu.VMEM),
        out_shape=jax.ShapeDtypeStruct((ROWS, LANES), bf16),
        scratch_shapes=[
            *buffers,
            pltpu.SemaphoreType.DMA((len(operands) - 1 + SEQS,)),
            pltpu.VMEM((3, SEQS, LANES), f32),
            pltpu.VMEM((SEQS * HEADS, HD), f32),
            pltpu.VMEM((SEQS, HEADS, HD), f32),
            pltpu.VMEM((HD, RANK), bf16),
            pltpu.VMEM((HALF, TOKENS), f32),
            pltpu.VMEM((HALF, TOKENS), f32),
            pltpu.VMEM((CHUNKS, LANES), jnp.int32),
            pltpu.VMEM((ROWS, LANES), f32),
            pltpu.VMEM((ROWS, LANES), f32),
            pltpu.VMEM((ROWS, LANES), f32),
            pltpu.VMEM((CHUNKS, LANES * SPAN), f32),
            pltpu.VMEM((SEQS * HEADS, TOKENS), f32),
            pltpu.VMEM((TOKENS, LANES), f32),
            pltpu.VMEM((SEQS * HD, TOKENS), bf16),
        ],
        compiler_params=pltpu.CompilerParams(vmem_limit_bytes=32 << 20),
        name="score",
    )(*[pltpu.with_memory_space_constraint(x, pltpu.HBM) for x in operands])


def weigh(packed, values):
    return pl.pallas_call(
        owner_kernel,
        in_specs=[pl.BlockSpec(memory_space=pltpu.VMEM)] * 2,
        out_specs=pl.BlockSpec(memory_space=pltpu.VMEM),
        out_shape=jax.ShapeDtypeStruct((PAIRS, SEQS, HEADS * HD), bf16),
        scratch_shapes=[
            pltpu.VMEM((1, ROWS), jnp.int32),
            pltpu.SMEM((1, ROWS), jnp.int32),
            pltpu.SemaphoreType.DMA,
            pltpu.VMEM((ROWS * SPAN, HD), f32),
            pltpu.VMEM((SEQS * HEADS, ROWS * SPAN), bf16),
            pltpu.VMEM((SEQS * HEADS, HD), f32),
        ],
        compiler_params=pltpu.CompilerParams(vmem_limit_bytes=24 << 20),
        name="weigh",
    )(packed, values)


def combine(gathered, weights, groups):
    return pl.pallas_call(
        combine_kernel,
        in_specs=[pl.BlockSpec(memory_space=pltpu.VMEM)] * 3,
        out_specs=pl.BlockSpec(memory_space=pltpu.VMEM),
        out_shape=jax.ShapeDtypeStruct((2 * groups, SEQS, LANES), f32),
        compiler_params=pltpu.CompilerParams(vmem_limit_bytes=16 << 20),
        name="combine",
    )(gathered, *weights)


def finish(parts, width):
    return pl.pallas_call(
        finish_kernel,
        in_specs=[pl.BlockSpec(memory_space=pltpu.VMEM)],
        out_specs=pl.BlockSpec(memory_space=pltpu.VMEM),
        out_shape=jax.ShapeDtypeStruct((SEQS, width), bf16),
        compiler_params=pltpu.CompilerParams(vmem_limit_bytes=8 << 20),
        name="finish",
    )(parts)


def on_device(query, query_pos, key_latent, key_up, value_cache, chosen, value_slot, out_weight):
    row_table, column_table = angle_tables()
    latent = jnp.swapaxes(key_latent, 1, 2)
    slot_rows = value_slot.reshape(-1, LANES)
    weights = [out_weight, lax.ppermute(out_weight, "side", [(0, 1), (1, 0)])]
    packed = score(query_pos, query, latent, key_up, chosen, slot_rows, row_table, column_table)
    arrived = lax.all_to_all(packed.reshape(POOLS, CAP, LANES), ("xb", "side", "z"), split_axis=0, concat_axis=0, tiled=True)
    arrived, weights[1] = lax.optimization_barrier((arrived, weights[1]))
    partial = weigh(arrived.reshape(ROWS, LANES), value_cache)
    gathered = lax.all_to_all(partial, ("xb", "z"), split_axis=0, concat_axis=0, tiled=True)
    groups = lax.axis_size("head")
    projected = combine(gathered, weights, groups)
    parts = lax.all_to_all(projected, ("side", "head"), split_axis=0, concat_axis=0, tiled=True)
    return finish(parts, out_weight.shape[1] // groups)


def solution(mesh):
    split = Mesh(mesh.devices.reshape(8, 2, 2, -1), ("z", "xb", "side", "head"))
    placed = (
        P(None, "head"),
        P(),
        P(None, ("z", "xb", "side"), None),
        P(None, "head"),
        P(("z", "xb", "side"), None, "head"),
        P(),
        P(),
        P("head", ("z", "xb", "side")),
    )
    return jax.shard_map(
        on_device, mesh=split, in_specs=placed, out_specs=P(None, ("z", "xb", "side", "head")), check_vma=False
    )
```
